128 devices in a mesh: lon: 32 (over z, x, core), lat: 4 (over y).
Axes of the slice: x: 4, y: 4, z: 4, core: 2. Of those that a mesh axis runs over, the one named last changes fastest.
Arguments:
- courant: float32 [4, 2, 137, 128, 512], P(None, None, None, 'lon', 'lat'), may hold values from -0.45 to 0.45
- slot_column_cells: int32 [4, 128, 128, 4], P(None, ('lon', 'lat')), may hold values from 0 to 511
- column_counts: int32 [4, 128, 128], P(None, ('lon', 'lat')), may hold values from 1 to 4, as said below
- innovations: float32 [4, 128, 128, 4, 128], P(None, ('lon', 'lat')), may hold values from -6 to 6
- error_weight: float32 [4, 128, 128, 4, 128], P(None, ('lon', 'lat')), may hold values from 0.3 to 3
- weighting: float32 [274, 128], replicated, may hold values from -0.375 to 0.375
Outputs:
- solution: float32 [2, 137, 128, 512], P(None, None, 'lon', 'lat')
- residual: float32 [2, 137, 128, 512], P(None, None, 'lon', 'lat')
The draws below stay inside these ranges and needn't reach their ends.
Inputs may be any that keep to these rules, and one draw needn't show every extreme that they name: `slot_column_cells`: A cell of the sending device's block, numbered longitude-major over its 4 x 128 cells; only slots below the matching count are read. `column_counts`: at every timestep some owner receives 4 live slots from every sending device.
All inputs are finite; a program needn't handle non-finite values.
Results may differ from the reference program's by a relative error of at most 0.00016.
Values sent between devices are 32-bit elements; how exact they have to be, the bound alone decides.
No kernel may reach another device: no remote copies, remote signals or barrier semaphores. Data moves between devices by JAX's collectives and lax.ppermute only.
A program may use at most 128 MiB of HBM per device.

```python
import math
import jax
import jax.numpy as jnp
from jax import lax

LEV = 137
CHAN = 128
NT = 4
ITERS = 2
CAP = 4
LONC = 4
LATC = 128
NLON = 128
NLAT = 512
CELLS = 512
N_LAT = 4
DEVICES = 128


def draw_column_counts(key, part):
    level_key = jax.random.fold_in(key, 11)
    count_key = jax.random.fold_in(key, 12)
    owner_key = jax.random.fold_in(key, 13)
    ceiling = jnp.minimum(jnp.power(2, jax.random.randint(level_key, (1, 1, DEVICES), 1, 3)), CAP)
    counts = jax.random.randint(count_key, (NT, DEVICES, DEVICES), ceiling // 2, ceiling + 1)
    crowded = jax.random.randint(owner_key, (NT, 1, 1), 0, DEVICES)
    owner_index = lax.broadcasted_iota(jnp.int32, (NT, DEVICES, DEVICES), 2)
    return jnp.where(owner_index == crowded, CAP, counts).astype(jnp.int32)


def set_ends(values, own_key, low, top_value):
    longest = values.shape.index(max(values.shape))
    spots = []
    for shift in (0, 1):
        where = [jax.random.randint(jax.random.fold_in(own_key, axis), (), 0, length) for axis, length in enumerate(values.shape)]
        where[longest] = (where[longest] + shift) % values.shape[longest]
        spots.append(tuple(where))
    return values.at[spots[0]].set(low).at[spots[1]].set(top_value)


def shard_levels(key, dims, shards, low, high):
    level = 1.0
    for dim, shards_of in shards:
        draws = jax.random.uniform(jax.random.fold_in(jax.random.fold_in(key, 6), dim), (shards_of,), jnp.float32, low / len(shards), high / len(shards))
        level = level * jnp.repeat(jnp.exp(draws), dims[dim] // shards_of).reshape((-1,) + (1,) * (len(dims) - 1 - dim))
    return level


def gaussian(stream_key, dims, deviation, reach, split=(), dtype=jnp.bfloat16):
    factor_of = shard_levels(stream_key, dims, split, -0.22, 0.18) if split else 1.0
    array = jax.random.normal(stream_key, dims, jnp.float32) * deviation * factor_of
    return jnp.minimum(jnp.maximum(array, -reach), reach).astype(dtype)


def setup_inputs(seed: int = 0) -> dict:
    streams_of = jax.random.split(jax.random.key(seed), 7)
    courant = jnp.clip(jax.random.uniform(streams_of[0], (NT, 2, LEV, NLON, NLAT), jnp.float32, -0.45, 0.45) * shard_levels(streams_of[0], (NT, 2, LEV, NLON, NLAT), ((3, 32), (4, 4)), -0.4, 0.0), -0.45, 0.45)
    slot_column_cells = set_ends(jax.random.randint(streams_of[1], (NT, DEVICES, DEVICES, CAP), 0, CELLS), jax.random.fold_in(streams_of[1], 1), 0, CELLS - 1).astype(jnp.int32)
    column_counts = draw_column_counts(jax.random.fold_in(streams_of[6], 71), 0)
    innovations = gaussian(streams_of[3], (NT, DEVICES, DEVICES, CAP, CHAN), 1.0, 6.0, ((1, 128),), jnp.float32)
    error_weight = jnp.clip(jnp.exp(math.log(3.0) - 2.3025851 * jax.random.uniform(streams_of[4], (NT, DEVICES, DEVICES, CAP, CHAN), jnp.float32) ** shard_levels(streams_of[4], (NT, DEVICES, DEVICES, CAP, CHAN), ((1, 128),), -0.2, 0.2)), 0.3, 3.0)
    weighting = gaussian(streams_of[5], (2 * LEV, CHAN), (2 * LEV) ** -0.5, 0.375, (), jnp.float32)
    return {"courant": courant, "slot_column_cells": slot_column_cells, "column_counts": column_counts, "innovations": innovations, "error_weight": error_weight, "weighting": weighting}


def advance(states, east_courant, north_courant):
    from_west = jnp.roll(states, 1, axis=2)
    from_east = jnp.roll(states, -1, axis=2)
    padded = jnp.pad(states, ((0, 0), (0, 0), (0, 0), (1, 1)))
    result = (1.0 - jnp.abs(east_courant) - jnp.abs(north_courant)) * states
    result = result + jnp.maximum(east_courant, 0.0) * from_west
    result = result + jnp.maximum(-east_courant, 0.0) * from_east
    result = result + jnp.maximum(north_courant, 0.0) * padded[:, :, :, :-2]
    result = result + jnp.maximum(-north_courant, 0.0) * padded[:, :, :, 2:]
    return result


def retreat(states, east_courant, north_courant):
    widths = ((0, 0), (0, 0), (0, 0), (1, 1))
    eastward = jnp.maximum(east_courant, 0.0) * states
    westward = jnp.maximum(-east_courant, 0.0) * states
    northward = jnp.pad(jnp.maximum(north_courant, 0.0) * states, widths)
    southward = jnp.pad(jnp.maximum(-north_courant, 0.0) * states, widths)
    result = (1.0 - jnp.abs(east_courant) - jnp.abs(north_courant)) * states
    result = result + jnp.roll(eastward, -1, axis=2)
    result = result + jnp.roll(westward, 1, axis=2)
    result = result + northward[:, :, :, 2:]
    result = result + southward[:, :, :, :-2]
    return result


def reference(courant, slot_column_cells, column_counts, innovations, error_weight, weighting):
    column_depth = 2 * LEV
    cell_total = NLON * NLAT
    highest = lax.Precision.HIGHEST
    sources = lax.broadcasted_iota(jnp.int32, (NT, DEVICES, DEVICES, CAP), 1)
    longitude = (sources // N_LAT) * LONC + slot_column_cells // LATC
    latitude = (sources % N_LAT) * LATC + slot_column_cells % LATC
    flat_index = (longitude * NLAT + latitude).astype(jnp.int32)
    slot_position = lax.broadcasted_iota(jnp.int32, (NT, DEVICES, DEVICES, CAP), 3)
    active = (slot_position < column_counts[:, :, :, None]).astype(jnp.float32)

    def observe(states, time_moment):
        columns = states.reshape(column_depth, cell_total)[:, flat_index[time_moment]]
        columns = columns * active[time_moment]
        return jnp.einsum("kgoc,kh->ogch", columns, weighting, precision=highest)

    def deposit(weighted, time_moment):
        gradient = jnp.einsum("ogch,kh->kgoc", weighted, weighting, precision=highest) * active[time_moment]
        total = jnp.zeros((column_depth, cell_total), jnp.float32)
        total = total.at[:, flat_index[time_moment].reshape(-1)].add(gradient.reshape(column_depth, -1))
        return total.reshape(2, LEV, NLON, NLAT)

    def tangent(states):
        payloads = []
        for time_moment in range(NT):
            states = advance(states, courant[time_moment, 0], courant[time_moment, 1])
            payloads.append(error_weight[time_moment] * observe(states, time_moment))
        return payloads

    def adjoint_sweep(payloads):
        sensitivity = jnp.zeros((2, LEV, NLON, NLAT), jnp.float32)
        for time_moment in reversed(range(NT)):
            sensitivity = sensitivity + deposit(payloads[time_moment], time_moment)
            sensitivity = retreat(sensitivity, courant[time_moment, 0], courant[time_moment, 1])
        return sensitivity

    def hessian(direction):
        return direction + adjoint_sweep(tangent(direction))

    weighted_all = error_weight * innovations
    right_hand_side = adjoint_sweep([weighted_all[time_moment] for time_moment in range(NT)])
    solution = jnp.zeros((2, LEV, NLON, NLAT), jnp.float32)
    residual = right_hand_side
    direction = right_hand_side
    residual_norm = jnp.sum(residual * residual)
    for iteration in range(ITERS):
        hessian_image = hessian(direction)
        step_length = residual_norm / jnp.sum(direction * hessian_image)
        solution = solution + step_length * direction
        residual = residual - step_length * hessian_image
        if iteration + 1 < ITERS:
            updated = jnp.sum(residual * residual)
            direction = residual + (updated / residual_norm) * direction
            residual_norm = updated
    return solution, residual
```

```python
import functools

import jax
import jax.numpy as jnp
from jax import lax
from jax.experimental import pallas as pl
from jax.experimental.pallas import tpu as pltpu
from jax.sharding import PartitionSpec as P

F32 = jnp.float32
BF16 = jnp.bfloat16
NT = 4
SLAB = 4
BAND = 128
EXT = 3 * SLAB
PLANES = {(0, 1): 0, (0, 2): 1, (0, 3): 2, (1, 1): 3, (1, 2): 4, (2, 1): 5}
VMEM = pl.BlockSpec(memory_space=pltpu.VMEM)
SMEM = pl.BlockSpec(memory_space=pltpu.SMEM)


def call(kernel, shapes, inputs, scratch=(), specs=None, flops=0):
    nbytes = sum(x.size * x.dtype.itemsize for x in inputs)
    return pl.pallas_call(
        kernel,
        out_shape=[jax.ShapeDtypeStruct(s, F32) for s in shapes],
        in_specs=specs or [VMEM] * len(inputs),
        out_specs=[VMEM] * len(shapes),
        scratch_shapes=list(scratch),
        compiler_params=pltpu.CompilerParams(vmem_limit_bytes=40 << 20),
        cost_estimate=pl.CostEstimate(flops=flops, bytes_accessed=nbytes, transcendentals=0),
    )(*inputs)


def turn(x, shift):
    shift %= 128
    return pltpu.roll(x, shift, x.ndim - 1) if shift else x


def lanes(shape=(8, 128)):
    return lax.broadcasted_iota(jnp.int32, shape, len(shape) - 1)


def parts(u):
    plus = jnp.maximum(u, 0.0)
    return plus, plus - u


def factors(u, v):
    up, um = parts(u)
    vp, vm = parts(v)
    return 1.0 - (up + um) - (vp + vm), up, um, vp, vm


def coefficients(refs, t, e, rows):
    own, west, east = refs[:3]
    if e < SLAB:
        k = 2 * PLANES[t, SLAB - e]
        return west[k, rows], west[k + 1, rows]
    if e >= 2 * SLAB:
        k = 2 * PLANES[t, e - 2 * SLAB + 1]
        return east[k, rows], east[k + 1, rows]
    k = 8 * t + e - SLAB
    return own[k, rows], own[k + SLAB, rows]


def pack_coefficients(refs, t, rows, group):
    own, west, east = refs[3:]
    out = []
    for k in (0, 1):
        p = jnp.where(group < 4, turn(west[k, rows], -32 * t), turn(own[k, rows], 32 - 32 * t))
        p = jnp.where(group < 8, p, turn(east[k, rows], 64 - 32 * t))
        out.append(jnp.where(group < 12, p, 0.0))
    return out


def adjoint_sweep(coef, grads, out_own, out_west, out_east, out_pack, levels):
    def block(r, carry):
        r8 = pl.multiple_of(r * 8, 8)
        rows = pl.ds(r8, 8)
        lane = lanes()
        group, off = lane // 8, lane % 8
        low, high = lane == 0, lane == BAND - 1
        ys = [[None] * EXT, [None] * EXT]
        packs = [None, None]
        for t in reversed(range(NT)):
            first, last = t + 1, 10 - t
            for var in (0, 1):
                for e in range(SLAB, 2 * SLAB):
                    g = grads[t, pl.ds(pl.multiple_of(var * levels + r8, 8), 8), pl.ds((e - SLAB) * BAND, BAND)]
                    ys[var][e] = g if ys[var][e] is None else ys[var][e] + g
            news = [[None] * EXT, [None] * EXT]
            tts = [jnp.zeros((8, 128), F32)] * 2
            mixes, pouts = [None, None], [None, None]
            if t < NT - 1:
                pu, pv = pack_coefficients(coef, t, rows, group)
                c0, up, um, vp, vm = factors(pu, pv)
                for var in (0, 1):
                    p = packs[var]
                    a, b = vp * p, vm * p
                    mixes[var] = jnp.where(off == 4, a, b)
                    pouts[var] = (c0 * p + turn(up * p, -8) + turn(um * p, 8), a, b)

            def put(var, e, x):
                news[var][e] = x if news[var][e] is None else news[var][e] + x

            for e in range(first, last + 1):
                c0, up, um, vp, vm = factors(*coefficients(coef, t, e, rows))
                for var in (0, 1):
                    y = ys[var][e]
                    if y is None:
                        continue
                    a, b = vp * y, vm * y
                    edge = 0.0 if mixes[var] is None else turn(mixes[var], -(8 * e + 4))
                    here = c0 * y + turn(jnp.where(low, edge, a), -1) + turn(jnp.where(high, edge, b), 1)
                    put(var, e, here)
                    put(var, e - 1, up * y)
                    put(var, e + 1, um * y)
                    mixed = turn(jnp.where(low, a, b), 8 * e + 4)
                    tts[var] = jnp.where((lane == 8 * e + 3) | (lane == 8 * e + 4), mixed, tts[var])
            for var in (0, 1):
                if pouts[var] is None:
                    packs[var] = turn(jnp.where(off == 4, tts[var], 0.0), -1) + turn(jnp.where(off == 3, tts[var], 0.0), 1)
                else:
                    rest, a, b = pouts[var]
                    packs[var] = rest + turn(jnp.where(off == 4, tts[var], a), -1) + turn(jnp.where(off == 3, tts[var], b), 1)
            ys = news
        for var in (0, 1):
            for e in range(SLAB):
                out_west[2 * e + var, rows] = ys[var][e]
                out_own[2 * e + var, rows] = ys[var][SLAB + e]
                out_east[2 * e + var, rows] = ys[var][2 * SLAB + e]
            out_west[2 * SLAB + var, rows] = packs[var]
            out_east[2 * SLAB + var, rows] = packs[var]
            out_pack[var, rows] = packs[var]
        return carry

    lax.fori_loop(0, levels // 8, block, 0)


def forward_sweep(coef, mains, smalls, fields, out_own, levels):
    def block(r, square):
        r8 = pl.multiple_of(r * 8, 8)
        rows = pl.ds(r8, 8)
        lane = lanes()
        group, off = lane // 8, lane % 8
        low, high = lane == 0, lane == BAND - 1
        rim = (lane < 4) | (lane >= BAND - 4)
        xs, packs = [[None] * EXT, [None] * EXT], [None, None]
        for var in (0, 1):
            pieces = [small[var, rows] for small in smalls]
            for e in range(EXT):
                source = (1, 0, 2)[e // SLAB]
                plane = mains[source][2 * (e % SLAB) + var, rows]
                fix = turn(pieces[source], -(8 * (SLAB + e % SLAB) + 4))
                xs[var][e] = plane + jnp.where(rim, fix, 0.0)
            p = jnp.where(group < 4, turn(pieces[1], -64), turn(pieces[0], -32))
            p = jnp.where(group < 8, p, pieces[2])
            packs[var] = jnp.where(group < 12, p, 0.0)
            for e in range(SLAB):
                x = xs[var][SLAB + e]
                out_own[2 * e + var, rows] = x
                square = square + x * x
        for t in range(NT):
            first, last = t + 1, 10 - t
            news = [[None] * EXT, [None] * EXT]
            tts = [jnp.zeros((8, 128), F32)] * 2
            for e in range(first, last + 1):
                c0, up, um, vp, vm = factors(*coefficients(coef, t, e, rows))
                for var in (0, 1):
                    x = xs[var][e]
                    edge = turn(packs[var], -(8 * e + 4))
                    news[var][e] = (
                        c0 * x
                        + up * xs[var][e - 1]
                        + um * xs[var][e + 1]
                        + vp * turn(jnp.where(high, edge, x), 1)
                        + vm * turn(jnp.where(low, edge, x), -1)
                    )
                    if t < NT - 1:
                        tts[var] = jnp.where((lane == 8 * e + 3) | (lane == 8 * e + 4), turn(x, 8 * e + 4), tts[var])
            if t < NT - 1:
                pu, pv = pack_coefficients(coef, t, rows, group)
                c0, up, um, vp, vm = factors(pu, pv)
                for var in (0, 1):
                    p = packs[var]
                    packs[var] = (
                        c0 * p
                        + up * turn(p, 8)
                        + um * turn(p, -8)
                        + vp * turn(jnp.where(off == 3, tts[var], p), 1)
                        + vm * turn(jnp.where(off == 4, tts[var], p), -1)
                    )
            xs = news
            for var in (0, 1):
                for e in range(SLAB, 2 * SLAB):
                    fields[t, pl.ds(pl.multiple_of(var * levels + r8, 8), 8), pl.ds((e - SLAB) * BAND, BAND)] = xs[var][e]
        return square

    return lax.fori_loop(0, levels // 8, block, jnp.zeros((8, 128), F32))


def halves(x):
    big = x.astype(BF16)
    return big, (x - big.astype(F32)).astype(BF16)


def dot(a, b):
    return jnp.dot(a, b, preferred_element_type=F32)


def split_dot(a_big, a_small, b):
    b_big, b_small = halves(b)
    return dot(a_big, b_big) + (dot(a_small, b_big) + dot(a_big, b_small))


def courant_kernel(levels, courant, own, to_west, to_east, edges):
    depth = courant.shape[0] // (2 * NT * SLAB)
    lane = lanes((levels, 128))
    for k in (0, 1):
        edge = jnp.zeros((levels, 128), F32)
        for t in range(NT):
            for l in range(SLAB):
                plane = 8 * t + 4 * k + l
                own[plane, pl.ds(levels - 8, 8)] = jnp.zeros((8, 128), F32)
                own[plane, pl.ds(0, depth)] = courant[pl.ds((2 * t + k) * depth * SLAB + l, depth, stride=SLAB)]
                x = own[plane]
                if t < NT - 1:
                    g = 4 * t + l
                    edge = jnp.where(lane // 8 == g, turn(x, 8 * g + 4), edge)
                    if l < NT - 1 - t:
                        to_west[2 * PLANES[t, l + 1] + k] = x
                    if l > t:
                        to_east[2 * PLANES[t, SLAB - l] + k] = x
        edges[k] = edge


def right_side_kernel(levels, cells, sent, index, weighting, *rest):
    coef, rest = rest[:6], rest[6:]
    out_own, out_west, out_east, out_pack, weights, grads = rest
    w_big, w_small = halves(weighting[...])
    count = index.shape[1]
    place = lax.broadcasted_iota(jnp.int32, (cells, count), 0)
    for t in range(NT):
        hit = jnp.where(place == index[pl.ds(t, 1), :], 1.0, 0.0).astype(BF16)
        a_big, a_small = halves(sent[t])
        b_big, b_small = halves(sent[NT + t])
        total = dot(hit, jnp.concatenate([a_big, b_big], 1)) + dot(hit, jnp.concatenate([a_small, b_small], 1))
        weights[t] = total[:, 128:].T
        grads[t] = split_dot(w_big, w_small, total[:, :128].T)
    adjoint_sweep(coef, grads, out_own, out_west, out_east, out_pack, levels)


def hessian_kernel(levels, mains, smalls, weights, weighting, columns, moments, *rest):
    coef, rest = rest[:6], rest[6:]
    out_own, out_west, out_east, out_pack, out_field, out_moments, fields = rest
    square = forward_sweep(coef, mains, smalls, fields, out_field, levels)
    w_big, w_small = halves(weighting[...])
    t_big, t_small = halves(columns[...])
    product = jnp.zeros((8, 128), F32)
    for t in range(NT):
        seen = split_dot(t_big, t_small, fields[t])
        weighed = weights[t] * seen
        product = product + jnp.sum((weighed * seen).reshape(-1, 8, SLAB, 128), axis=(0, 2))
        fields[t] = split_dot(w_big, w_small, weighed)
    lane = lanes(out_moments.shape)
    before = moments[pl.ds(0, 1), :]
    found = jnp.where(lane == 2, jnp.sum(square), jnp.where(lane == 3, jnp.sum(product), 0.0))
    out_moments[...] = jnp.where(lane < 2, turn(jnp.broadcast_to(before, lane.shape), -2), found)
    adjoint_sweep(coef, fields, out_own, out_west, out_east, out_pack, levels)


def hessian_entry(levels, own, west, east, s_own, s_west, s_east, *rest):
    hessian_kernel(levels, (own, west, east), (s_own, s_west, s_east), *rest)


def gather_kernel(own, pack, from_west, from_east, main, message, aligned):
    lane = lanes(pack.shape[1:])
    group = lane // 8
    for var in (0, 1):
        p = pack[var] + turn(from_east[2 * SLAB + var], 32) + turn(from_west[2 * SLAB + var], -32)
        out = jnp.where((group >= 4) & (group < 8), p, 0.0)
        for l in range(SLAB):
            k = 2 * l + var
            x = own[k] + from_west[k] + from_east[k]
            main[k] = x
            out = jnp.where(group == 8 + l, turn(x, 8 * (8 + l) + 4), out)
        message[var] = out
        aligned[var] = turn(p, 32)


def final_kernel(band, v0, v1, main, south, north, sums, solution, residual):
    total = jnp.sum(sums[...], axis=0, keepdims=True)
    lane = lanes(total.shape)
    m = [jnp.sum(jnp.where(lane == k, total, 0.0), axis=1, keepdims=True) for k in range(4)]
    a, c, d = m[1] / m[0], m[2] / m[0], m[3] / m[0]
    step0 = 1.0 / (1.0 + a)
    keep = a * step0
    ratio = (c - a * a) * step0 * step0
    p, s = keep + ratio, -step0
    curvature = p * p + 2.0 * p * s * a + s * s * c + (p * p * a + 2.0 * p * s * c + s * s * d)
    step1 = ratio / curvature
    depth = solution.shape[0] // (2 * SLAB)
    levels = main.shape[1]
    lane = lanes((levels, 128))
    rim, off = (lane < 4) | (lane >= BAND - 4), lane % 8
    where, bands = band[0], band[1]
    for var in (0, 1):
        fix = jnp.where(
            off < 4,
            jnp.where(where < bands - 1, north[var], 0.0),
            jnp.where(where > 0, south[var], 0.0),
        )
        for l in range(SLAB):
            k = 2 * l + var
            x0, x1 = v0[k], v1[k]
            x2 = main[k] + jnp.where(rim, turn(fix, -(8 * (SLAB + l) + 4)), 0.0)
            rows = pl.ds(var * depth * SLAB + l, depth, stride=SLAB)
            out = (step0 + step1 * p) * x0 + (step1 * s) * x1
            left = (keep - step1 * p) * x0 + (s - step1 * (p + s)) * x1 - (step1 * s) * x2
            solution[rows] = out[:depth]
            residual[rows] = left[:depth]


def shift(x, axis, by):
    n = lax.axis_size(axis)
    return lax.ppermute(x, axis, [(i, (i + by) % n) for i in range(n)])


def body(courant, slot_column_cells, column_counts, innovations, error_weight, weighting):
    depth = courant.shape[2]
    levels = -(-depth // 16) * 16
    owners = slot_column_cells.shape[2]
    capacity = slot_column_cells.shape[3]
    cells = SLAB * BAND
    channels = weighting.shape[1]
    bands = lax.axis_size("lat")
    band = lax.axis_index("lat")

    own, to_west, to_east, edges = call(
        functools.partial(courant_kernel, levels),
        [(2 * NT * SLAB, levels, 128), (12, levels, 128), (12, levels, 128), (2, levels, 128)],
        [courant.reshape(2 * NT * depth * SLAB, BAND)],
    )
    from_east, from_west = shift(to_west, "lon", -1), shift(to_east, "lon", 1)
    from_south, from_north = shift(edges, "lat", 1), shift(edges, "lat", -1)

    weights_here = error_weight[:, 0]
    sent = lax.all_to_all(
        jnp.concatenate([weights_here * innovations[:, 0], weights_here], 0),
        ("lon", "lat"),
        split_axis=1,
        concat_axis=1,
        tiled=True,
    ).reshape(2 * NT, owners * capacity, channels)
    slot = lax.broadcasted_iota(jnp.int32, (NT, owners, capacity), 2)
    index = jnp.where(slot < column_counts[:, 0, :, None], slot_column_cells[:, 0], -1).reshape(NT, owners * capacity)
    weighting_rows = jnp.pad(weighting.reshape(2, depth, channels), ((0, 0), (0, levels - depth), (0, 0))).reshape(
        2 * levels, channels
    )
    weighting_columns = weighting_rows.T

    lane = lanes((1, 1, 128))
    group, lower = lane // 8, lane % 8 < 4
    not_first, not_last = band > 0, band < bands - 1
    pack = jnp.where(
        lower,
        jnp.where(not_first, from_south, 0.0),
        jnp.where(not_last, from_north, 0.0),
    )
    coef = [own, from_west, from_east, pack, shift(pack, "lon", 1), shift(pack, "lon", -1)]

    planes, message = (2 * SLAB, levels, 128), (2 * SLAB + 2, levels, 128)
    small = (2, levels, 128)
    grads = pltpu.VMEM((NT, 2 * levels, cells), F32)

    def gathered(parts):
        mine, to_west, to_east, pack = parts
        return call(
            gather_kernel,
            [planes, small, small],
            [mine, pack, shift(to_east, "lon", 1), shift(to_west, "lon", -1)],
        )

    def hessian(state, weights, moments, rows):
        main, message_lat, aligned = state
        main_west, main_east = shift(main, "lon", 1), shift(main, "lon", -1)
        south, north = shift(message_lat, "lat", 1), shift(message_lat, "lat", -1)
        outer = aligned + jnp.where(lower, south, north)
        inner = jnp.where(lower, north, south)
        edge = jnp.where(
            (group >= 8) & (group < 12),
            jnp.where(jnp.where(lower, not_first, not_last), outer, 0.0),
            jnp.where(jnp.where(lower, not_last, not_first) & (group >= 4) & (group < 8), inner, 0.0),
        )
        return call(
            functools.partial(hessian_entry, levels),
            [planes, message, message, small, planes, (rows, 128)],
            [
                main, main_west, main_east, edge, shift(edge, "lon", 1), shift(edge, "lon", -1),
                weights, weighting_rows, weighting_columns, moments, *coef,
            ],
            [grads],
        )

    *parts, weights = call(
        functools.partial(right_side_kernel, levels, cells),
        [planes, message, message, small, (NT, channels, cells)],
        [sent, index, weighting_rows, *coef],
        [grads],
    )
    *parts, v0, moments = hessian(gathered(parts), weights, jnp.zeros((8, 128), F32), 8)
    *parts, v1, moments = hessian(gathered(parts), weights, moments, owners)
    sums = lax.all_to_all(moments, ("lon", "lat"), split_axis=0, concat_axis=0, tiled=True)
    main, message_lat, _ = gathered(parts)
    solution, residual = call(
        final_kernel,
        [(2 * depth * SLAB, BAND)] * 2,
        [
            jnp.stack([band, jnp.int32(bands)]).astype(jnp.int32),
            v0, v1, main, shift(message_lat, "lat", 1), shift(message_lat, "lat", -1), sums,
        ],
        specs=[SMEM] + [VMEM] * 6,
    )
    shape = (2, depth, SLAB, BAND)
    return solution.reshape(shape), residual.reshape(shape)


def solution(mesh):
    in_specs = (
        P(None, None, None, "lon", "lat"),
        P(None, ("lon", "lat"), None, None),
        P(None, ("lon", "lat"), None),
        P(None, ("lon", "lat"), None, None, None),
        P(None, ("lon", "lat"), None, None, None),
        P(),
    )
    out_specs = (P(None, None, "lon", "lat"), P(None, None, "lon", "lat"))
    return jax.shard_map(body, mesh=mesh, in_specs=in_specs, out_specs=out_specs, check_vma=False)
```

```python
import functools

import jax
import jax.numpy as jnp
from jax import lax
from jax.experimental import pallas as pl
from jax.experimental.pallas import tpu as pltpu
from jax.sharding import PartitionSpec as P

F32 = jnp.float32
BF16 = jnp.bfloat16
NT = 4
SLAB = 4
BAND = 128
EXT = 3 * SLAB
SLOTS = 4
PLANES = {(0, 1): 0, (0, 2): 1, (0, 3): 2, (1, 1): 3, (1, 2): 4, (2, 1): 5}
VMEM = pl.BlockSpec(memory_space=pltpu.VMEM)
HBM = pl.BlockSpec(memory_space=pltpu.HBM)
SMEM = pl.BlockSpec(memory_space=pltpu.SMEM)


def call(kernel, shapes, inputs, scratch=(), flops=0, hbm_in=(), hbm_out=()):
    nbytes = sum(x.size * x.dtype.itemsize for x in inputs)
    return pl.pallas_call(
        kernel,
        out_shape=[jax.ShapeDtypeStruct(s, F32) for s in shapes],
        in_specs=[SMEM] + [HBM if i in hbm_in else VMEM for i in range(1, len(inputs))],
        out_specs=[HBM if i in hbm_out else VMEM for i in range(len(shapes))],
        scratch_shapes=list(scratch),
        compiler_params=pltpu.CompilerParams(vmem_limit_bytes=28 << 20),
        cost_estimate=pl.CostEstimate(flops=flops, bytes_accessed=nbytes, transcendentals=0),
    )(*inputs)


def turn(x, shift):
    shift %= 128
    return pltpu.roll(x, shift, x.ndim - 1) if shift else x


def lanes(shape=(8, 128)):
    return lax.broadcasted_iota(jnp.int32, shape, len(shape) - 1)


def flip(x, group):
    lane = lanes(x.shape)
    return jnp.take_along_axis(x, (8 * group + 3 - lane) & 127, axis=1, mode="promise_in_bounds")


def sides(odd, near, far):
    return jnp.where(odd, near, far), jnp.where(odd, far, near)


def parts(u):
    plus = jnp.maximum(u, 0.0)
    return plus, plus - u


def factors(u, v):
    up, um = parts(u)
    vp, vm = parts(v)
    return 1.0 - (up + um) - (vp + vm), up, um, vp, vm


def coefficients(odd, refs, t, e, rows):
    own, near, far = refs[:3]
    if SLAB <= e < 2 * SLAB:
        k = 8 * t + e - SLAB
        return own[k, rows], own[k + SLAB, rows]
    k = 2 * PLANES[t, SLAB - e if e < SLAB else e - 2 * SLAB + 1]
    side = 0 if e < SLAB else 1
    return tuple(sides(odd, near[k + i, rows], far[k + i, rows])[side] for i in (0, 1))


def pack_coefficients(odd, refs, t, rows, group):
    own, near, far = refs[3:]
    out = []
    for k in (0, 1):
        west, east = sides(odd, near[k, rows], far[k, rows])
        p = jnp.where(group < 4, turn(west, -32 * t), turn(own[k, rows], 32 - 32 * t))
        p = jnp.where(group < 8, p, turn(east, 64 - 32 * t))
        out.append(jnp.where(group < 12, p, 0.0))
    return out


def adjoint_sweep(odd, coef, grads, out_own, out_near, out_far, out_pack, levels):
    def block(r, carry):
        r8 = pl.multiple_of(r * 8, 8)
        rows = pl.ds(r8, 8)
        lane = lanes()
        group, off = lane // 8, lane % 8
        low, high = lane == 0, lane == BAND - 1
        ys = [[None] * EXT, [None] * EXT]
        packs = [None, None]
        for t in reversed(range(NT)):
            first, last = t + 1, 10 - t
            for var in (0, 1):
                for e in range(SLAB, 2 * SLAB):
                    g = grads[t, pl.ds(pl.multiple_of(var * levels + r8, 8), 8), pl.ds((e - SLAB) * BAND, BAND)]
                    ys[var][e] = g if ys[var][e] is None else ys[var][e] + g
            news = [[None] * EXT, [None] * EXT]
            tts = [jnp.zeros((8, 128), F32)] * 2
            mixes, pouts = [None, None], [None, None]
            if t < NT - 1:
                pu, pv = pack_coefficients(odd, coef, t, rows, group)
                c0, up, um, vp, vm = factors(pu, pv)
                for var in (0, 1):
                    p = packs[var]
                    a, b = vp * p, vm * p
                    mixes[var] = jnp.where(off == 3, a, b)
                    pouts[var] = (c0 * p + turn(up * p, -8) + turn(um * p, 8), turn(a, 1), turn(b, -1))

            def put(var, e, x):
                news[var][e] = x if news[var][e] is None else news[var][e] + x

            for e in range(first, last + 1):
                c0, up, um, vp, vm = factors(*coefficients(odd, coef, t, e, rows))
                for var in (0, 1):
                    y = ys[var][e]
                    a, b = vp * y, vm * y
                    edge = 0.0 if mixes[var] is None else turn(mixes[var], -(8 * e + 4))
                    put(var, e, c0 * y + jnp.where(high, edge, turn(a, -1)) + jnp.where(low, edge, turn(b, 1)))
                    put(var, e - 1, up * y)
                    put(var, e + 1, um * y)
                    mixed = turn(jnp.where(low, a, b), 8 * e + 4)
                    tts[var] = jnp.where((lane == 8 * e + 3) | (lane == 8 * e + 4), mixed, tts[var])
            for var in (0, 1):
                rest, a, b = (0.0, 0.0, 0.0) if pouts[var] is None else pouts[var]
                packs[var] = rest + (jnp.where(off == 4, tts[var], a) + jnp.where(off == 3, tts[var], b))
            ys = news
        for var in (0, 1):
            for e in range(SLAB):
                k = 2 * e + var
                west, east = ys[var][e], ys[var][2 * SLAB + e]
                out_own[k, rows] = ys[var][SLAB + e]
                out_near[k, rows] = jnp.where(odd, west, east)
                out_far[k, rows] = jnp.where(odd, east, west)
            out_pack[var, rows] = packs[var]
        both = jnp.where((group & 4) == 0, packs[0], turn(packs[1], 32))
        out_near[2 * SLAB, rows] = both
        out_far[2 * SLAB, rows] = both
        return carry

    lax.fori_loop(0, levels // 8, block, 0, unroll=2)


def forward_sweep(odd, coef, mains, smalls, fields, out_own, levels):
    def block(r, square):
        r8 = pl.multiple_of(r * 8, 8)
        rows = pl.ds(r8, 8)
        lane = lanes()
        group, off = lane // 8, lane % 8
        low, high = lane == 0, lane == BAND - 1
        rim = (lane < 4) | (lane >= BAND - 4)
        xs, packs = [[None] * EXT, [None] * EXT], [None, None]
        pieces = (smalls[0][rows], *sides(odd, smalls[1][rows], smalls[2][rows]))
        for var in (0, 1):
            for l in range(SLAB):
                k = 2 * l + var
                planes = (mains[0][k, rows], *sides(odd, mains[1][k, rows], mains[2][k, rows]))
                for part, e in ((0, SLAB + l), (1, l), (2, 2 * SLAB + l)):
                    xs[var][e] = planes[part] + jnp.where(rim, flip(pieces[part], 8 * var + l), 0.0)
            p = jnp.where(group < 4, turn(pieces[1], -64 * var - 32), turn(pieces[0], -64 * var))
            p = jnp.where(group < 8, p, turn(pieces[2], 32 - 64 * var))
            packs[var] = jnp.where(group < 12, p, 0.0)
            for l in range(SLAB):
                x = xs[var][SLAB + l]
                out_own[2 * l + var, rows] = x
                square = square + x * x
        for t in range(NT):
            first, last = t + 1, 10 - t
            news = [[None] * EXT, [None] * EXT]
            tts = [jnp.zeros((8, 128), F32)] * 2
            for e in range(first, last + 1):
                c0, up, um, vp, vm = factors(*coefficients(odd, coef, t, e, rows))
                for var in (0, 1):
                    x = xs[var][e]
                    edge = turn(packs[var], -(8 * e + 4))
                    news[var][e] = (
                        c0 * x
                        + up * xs[var][e - 1]
                        + um * xs[var][e + 1]
                        + vp * jnp.where(low, edge, turn(x, 1))
                        + vm * jnp.where(high, edge, turn(x, -1))
                    )
                    if t < NT - 1:
                        tts[var] = jnp.where((lane == 8 * e + 3) | (lane == 8 * e + 4), turn(x, 8 * e + 4), tts[var])
            if t < NT - 1:
                pu, pv = pack_coefficients(odd, coef, t, rows, group)
                c0, up, um, vp, vm = factors(pu, pv)
                for var in (0, 1):
                    p = packs[var]
                    packs[var] = (
                        c0 * p
                        + up * turn(p, 8)
                        + um * turn(p, -8)
                        + vp * jnp.where(off == 3, tts[var], turn(p, -1))
                        + vm * jnp.where(off == 4, tts[var], turn(p, 1))
                    )
            xs = news
            for var in (0, 1):
                for e in range(SLAB, 2 * SLAB):
                    fields[t, pl.ds(pl.multiple_of(var * levels + r8, 8), 8), pl.ds((e - SLAB) * BAND, BAND)] = xs[var][e]
        return square

    return lax.fori_loop(0, levels // 8, block, jnp.zeros((8, 128), F32), unroll=2)


def halves(x):
    big = x.astype(BF16)
    return big, (x - big.astype(F32)).astype(BF16)


def dot(a, b):
    return jnp.dot(a, b, preferred_element_type=F32)


def split_dot(a_big, a_small, b):
    b_big, b_small = halves(b)
    return dot(a_big, b_big) + (dot(a_small, b_big) + dot(a_big, b_small))


def message_kernel(flags, given_weight, given, sent, error_weight, innovations, message, done):
    copies = [
        pltpu.make_async_copy(source, target, done.at[i])
        for i, (source, target) in enumerate(((given_weight, error_weight), (given, innovations)))
    ]
    for copy in copies:
        copy.start()
    for copy in copies:
        copy.wait()
    owners = error_weight.shape[0] // (NT * SLOTS)
    for t in range(NT):
        for c in range(SLOTS):
            here = pl.ds((t * owners) * SLOTS + c, owners, stride=SLOTS)
            weight = error_weight[here]
            message[pl.ds(t * SLOTS + c, owners, stride=2 * NT * SLOTS)] = weight * innovations[here]
            message[pl.ds((NT + t) * SLOTS + c, owners, stride=2 * NT * SLOTS)] = weight
    send = pltpu.make_async_copy(message, sent, done.at[2])
    send.start()
    send.wait()


def prepare_kernel(levels, flags, courant, weighting, *outs):
    own, to_near, to_far, edges, table, columns = outs
    depth = courant.shape[0] // (2 * NT * SLAB)
    odd = flags[0] == 1
    lane = lanes((levels, 128))
    for k in (0, 1):
        edge = jnp.zeros((levels, 128), F32)
        for t in range(NT):
            xs = []
            for l in range(SLAB):
                plane = 8 * t + 4 * k + l
                own[plane, pl.ds(levels - 8, 8)] = jnp.zeros((8, 128), F32)
                own[plane, pl.ds(0, depth)] = courant[pl.ds((2 * t + k) * depth * SLAB + l, depth, stride=SLAB)]
                xs.append(own[plane])
                if t < NT - 1:
                    g = 4 * t + l
                    edge = jnp.where(lane // 8 == g, flip(xs[l], g), edge)
            for d in range(1, NT - t):
                west, east = xs[d - 1], xs[SLAB - d]
                to_near[2 * PLANES[t, d] + k] = jnp.where(odd, west, east)
                to_far[2 * PLANES[t, d] + k] = jnp.where(odd, east, west)
        edges[k] = edge
        table[pl.ds(levels * (k + 1) - 8, 8)] = jnp.zeros((8, 128), F32)
        table[pl.ds(levels * k, depth)] = weighting[pl.ds(depth * k, depth)]
    columns[...] = table[...].T


def pack_kernel(flags, south, north, pack):
    lane = lanes(pack.shape)
    inside = jnp.where(flags[1] < flags[2] - 1, north[...], 0.0)
    pack[...] = jnp.where(lane % 8 < 4, inside, jnp.where(flags[1] > 0, south[...], 0.0))


def edge_kernel(flags, aligned, south, north, edge):
    lane = lanes(edge.shape)
    upper = lane % 8 < 4
    fix = jnp.where(
        upper,
        jnp.where(flags[1] > 0, south[...], 0.0),
        jnp.where(flags[1] < flags[2] - 1, north[...], 0.0),
    )
    halo = jnp.where(
        upper,
        jnp.where(flags[1] < flags[2] - 1, aligned[...] + north[...], 0.0),
        jnp.where(flags[1] > 0, aligned[...] + south[...], 0.0),
    )
    edge[...] = jnp.where(lane % 64 < 32, fix, halo)


def slots_kernel(cells, flags, sent, index, counts, table, weights, grads):
    w_big, w_small = halves(table[...])
    owners = counts.shape[1]
    place = lax.broadcasted_iota(jnp.int32, (cells, owners), 0)
    for t in range(NT):
        hits, bigs, smalls = [], [], []
        for c in range(SLOTS):
            slot = jnp.where(c < counts[pl.ds(t, 1), :], index[t, pl.ds(c, 1), :], -1)
            hits.append(jnp.where(place == slot, 1.0, 0.0).astype(BF16))
            both = [sent[pl.ds((i * NT + t) * SLOTS + c, owners, stride=2 * NT * SLOTS)] for i in (0, 1)]
            big, small = halves(jnp.concatenate(both, 1))
            bigs.append(big)
            smalls.append(small)
        hit = jnp.concatenate(hits, 1)
        total = dot(hit, jnp.concatenate(bigs, 0)) + dot(hit, jnp.concatenate(smalls, 0))
        weights[t] = total[:, 128:].T
        grads[t] = split_dot(w_big, w_small, total[:, :128].T)


def right_side_kernel(levels, flags, grads, *rest):
    coef, outs = rest[:6], rest[6:]
    adjoint_sweep(flags[0] == 1, coef, grads, *outs, levels)


def hessian_kernel(levels, flags, own, near, far, s_own, s_near, s_far, weights, table, columns, moments, *rest):
    coef, rest = rest[:6], rest[6:]
    out_own, out_near, out_far, out_pack, out_field, out_moments, fields = rest
    odd = flags[0] == 1
    square = forward_sweep(odd, coef, (own, near, far), (s_own, s_near, s_far), fields, out_field, levels)
    w_big, w_small = halves(table[...])
    t_big, t_small = halves(columns[...])
    product = jnp.zeros((8, 128), F32)
    for t in range(NT):
        seen = split_dot(t_big, t_small, fields[t])
        weighed = weights[t] * seen
        product = product + jnp.sum((weighed * seen).reshape(-1, 8, SLAB, 128), axis=(0, 2))
        fields[t] = split_dot(w_big, w_small, weighed)
    lane = lanes(out_moments.shape)
    before = moments[pl.ds(0, 1), :]
    found = jnp.where(lane == 2, jnp.sum(square), jnp.where(lane == 3, jnp.sum(product), 0.0))
    out_moments[...] = jnp.where(lane < 2, turn(jnp.broadcast_to(before, lane.shape), -2), found)
    adjoint_sweep(odd, coef, fields, out_own, out_near, out_far, out_pack, levels)


def gather_kernel(flags, own, pack, near, far, *rest):
    main, message, aligned = rest[-3:]
    lane = lanes(message.shape)
    group = lane // 8
    odd = flags[0] == 1
    west, east = sides(odd, near[2 * SLAB], far[2 * SLAB])
    out, left = jnp.zeros(message.shape, F32), jnp.zeros(message.shape, F32)
    for var in (0, 1):
        p = pack[var] + turn(east, 32 - 32 * var) + turn(west, -32 - 32 * var)
        out = jnp.where(group // 4 == 2 * var, turn(p, 64 * var - 32), out)
        left = jnp.where(group // 4 == 2 * var + 1, turn(p, 64 * var), left)
        for l in range(SLAB):
            k = 2 * l + var
            x = own[k] + (near[k] + far[k])
            main[k] = x
            g = 8 * var + SLAB + l
            out = jnp.where(group == g, flip(x, g), out)
    message[...] = out
    aligned[...] = left


def final_kernel(flags, v0, v1, main, south, north, sums, solution, residual):
    total = jnp.sum(sums[...], axis=0, keepdims=True)
    lane = lanes(total.shape)
    m = [jnp.sum(jnp.where(lane == k, total, 0.0), axis=1, keepdims=True) for k in range(4)]
    a, c, d = m[1] / m[0], m[2] / m[0], m[3] / m[0]
    step0 = 1.0 / (1.0 + a)
    keep = a * step0
    ratio = (c - a * a) * step0 * step0
    p, s = keep + ratio, -step0
    curvature = p * p + 2.0 * p * s * a + s * s * c + (p * p * a + 2.0 * p * s * c + s * s * d)
    step1 = ratio / curvature
    depth = solution.shape[0] // (2 * SLAB)
    lane = lanes(south.shape)
    rim = (lane < 4) | (lane >= BAND - 4)
    fix = jnp.where(
        lane % 8 < 4,
        jnp.where(flags[1] > 0, south[...], 0.0),
        jnp.where(flags[1] < flags[2] - 1, north[...], 0.0),
    )
    for var in (0, 1):
        for l in range(SLAB):
            k = 2 * l + var
            x0, x1 = v0[k], v1[k]
            x2 = main[k] + jnp.where(rim, flip(fix, 8 * var + l), 0.0)
            rows = pl.ds(var * depth * SLAB + l, depth, stride=SLAB)
            out = (step0 + step1 * p) * x0 + (step1 * s) * x1
            left = (keep - step1 * p) * x0 + (s - step1 * (p + s)) * x1 - (step1 * s) * x2
            solution[rows] = out[:depth]
            residual[rows] = left[:depth]


def shift(x, axis, by):
    n = lax.axis_size(axis)
    return lax.ppermute(x, axis, [(i, (i + by) % n) for i in range(n)])


def far_swap(x):
    n = lax.axis_size("lon")
    return lax.ppermute(x, "lon", [(i, (i + 1 if i % 2 else i - 1) % n) for i in range(n)])


def near_swap(x):
    return lax.ppermute(x, "lon", [(i, i ^ 1) for i in range(lax.axis_size("lon"))])


def body(courant, slot_column_cells, column_counts, innovations, error_weight, weighting):
    depth = courant.shape[2]
    levels = -(-depth // 16) * 16
    owners = slot_column_cells.shape[2]
    cells = SLAB * BAND
    channels = weighting.shape[1]
    flags = jnp.stack([lax.axis_index("lon") % 2, lax.axis_index("lat"), jnp.int32(lax.axis_size("lat"))]).astype(jnp.int32)
    slots = owners * SLOTS

    (message,) = call(
        message_kernel,
        [(2 * NT * slots, channels)],
        [flags, error_weight.reshape(NT * slots, channels), innovations.reshape(NT * slots, channels)],
        [
            pltpu.VMEM((NT * slots, channels), F32), pltpu.VMEM((NT * slots, channels), F32),
            pltpu.VMEM((2 * NT * slots, channels), F32), pltpu.SemaphoreType.DMA((3,)),
        ],
        hbm_in=(1, 2),
        hbm_out=(0,),
    )
    sent = lax.all_to_all(
        message.reshape(owners, 2 * NT * SLOTS, channels), ("lon", "lat"), split_axis=0, concat_axis=0, tiled=True
    ).reshape(2 * NT * slots, channels)
    own, to_near, to_far, edges, table, columns = call(
        functools.partial(prepare_kernel, levels),
        [
            (2 * NT * SLAB, levels, 128), (12, levels, 128), (12, levels, 128), (2, levels, 128),
            (2 * levels, channels), (channels, 2 * levels),
        ],
        [flags, courant.reshape(2 * NT * depth * SLAB, BAND), weighting],
    )
    c_far, c_near = far_swap(to_far), near_swap(to_near)
    (pack,) = call(pack_kernel, [(2, levels, 128)], [flags, shift(edges, "lat", 1), shift(edges, "lat", -1)])
    index = jnp.swapaxes(slot_column_cells[:, 0], 1, 2)
    coef = [own, c_near, c_far, pack, near_swap(pack), far_swap(pack)]

    planes, parcel = (2 * SLAB, levels, 128), (2 * SLAB + 1, levels, 128)
    small = (levels, 128)
    grads = pltpu.VMEM((NT, 2 * levels, cells), F32)
    pieces = [planes, parcel, parcel, (2, levels, 128)]

    def gathered(parts, *more):
        mine, to_near, to_far, pack = parts
        return call(
            gather_kernel, [planes, small, small], [flags, mine, pack, near_swap(to_near), far_swap(to_far), *more]
        )

    def hessian(state, weights, moments, rows):
        main, message, aligned = state
        (edge,) = call(edge_kernel, [small], [flags, aligned, shift(message, "lat", 1), shift(message, "lat", -1)])
        return call(
            functools.partial(hessian_kernel, levels),
            [*pieces, planes, (rows, 128)],
            [
                flags, main, near_swap(main), far_swap(main), edge, near_swap(edge), far_swap(edge),
                weights, table, columns, moments, *coef,
            ],
            [grads],
        )

    weights, right = call(
        functools.partial(slots_kernel, cells),
        [(NT, channels, cells), (NT, 2 * levels, cells)],
        [flags, sent, index, column_counts[:, 0], table],
    )
    parts = call(functools.partial(right_side_kernel, levels), pieces, [flags, right, *coef])
    *parts, v0, moments = hessian(gathered(parts), weights, jnp.zeros((8, 128), F32), 8)
    *parts, v1, moments = hessian(gathered(parts), weights, moments, owners)
    sums = lax.all_to_all(moments, ("lon", "lat"), split_axis=0, concat_axis=0, tiled=True)
    main, message, _ = gathered(parts, sums)
    solution, residual = call(
        final_kernel,
        [(2 * depth * SLAB, BAND)] * 2,
        [flags, v0, v1, main, shift(message, "lat", 1), shift(message, "lat", -1), sums],
    )
    shape = (2, depth, SLAB, BAND)
    return solution.reshape(shape), residual.reshape(shape)


def solution(mesh):
    in_specs = (
        P(None, None, None, "lon", "lat"),
        P(None, ("lon", "lat"), None, None),
        P(None, ("lon", "lat"), None),
        P(None, ("lon", "lat"), None, None, None),
        P(None, ("lon", "lat"), None, None, None),
        P(),
    )
    out_specs = (P(None, None, "lon", "lat"), P(None, None, "lon", "lat"))
    return jax.shard_map(body, mesh=mesh, in_specs=in_specs, out_specs=out_specs, check_vma=False)
```

```python
import functools

import jax
import jax.numpy as jnp
from jax import lax
from jax.experimental import pallas as pl
from jax.experimental.pallas import tpu as pltpu
from jax.sharding import PartitionSpec as P

F32 = jnp.float32
BF16 = jnp.bfloat16
NT = 4
SLAB = 4
BAND = 128
EXT = 3 * SLAB
SLOTS = 4
TILES = 17
ROWS = 8 * TILES
REST = 9
SHARE = SLAB * REST
BASE = (0, 10, 18, 24)
PLANES = {(0, 1): 0, (0, 2): 1, (0, 3): 2, (1, 1): 3, (1, 2): 4, (2, 1): 5}
VMEM = pl.BlockSpec(memory_space=pltpu.VMEM)
HBM = pl.BlockSpec(memory_space=pltpu.HBM)
SMEM = pl.BlockSpec(memory_space=pltpu.SMEM)


def call(kernel, shapes, inputs, scratch=(), flops=0, hbm_in=(), hbm_out=()):
    nbytes = sum(x.size * x.dtype.itemsize for x in inputs)
    return pl.pallas_call(
        kernel,
        out_shape=[jax.ShapeDtypeStruct(s, F32) for s in shapes],
        in_specs=[SMEM] + [HBM if i in hbm_in else VMEM for i in range(1, len(inputs))],
        out_specs=[HBM if i in hbm_out else VMEM for i in range(len(shapes))],
        scratch_shapes=list(scratch),
        compiler_params=pltpu.CompilerParams(vmem_limit_bytes=32 << 20),
        cost_estimate=pl.CostEstimate(flops=flops, bytes_accessed=nbytes, transcendentals=0),
    )(*inputs)


def turn(x, shift):
    shift %= 128
    return pltpu.roll(x, shift, 1) if shift else x


def drop(x, by):
    return pltpu.roll(x, by % 8, 0)


def lanes(shape=(8, 128)):
    return lax.broadcasted_iota(jnp.int32, shape, len(shape) - 1)


def depths():
    return lax.broadcasted_iota(jnp.int32, (8, 128), 0)


def tile(m):
    return pl.ds(8 * m, 8)


def parts(u):
    plus = jnp.maximum(u, 0.0)
    return plus, plus - u


def factors(u, v):
    up, um = parts(u)
    vp, vm = parts(v)
    return 1.0 - (up + um) - (vp + vm), up, um, vp, vm


def forward_sweep(main_c, left_c, xs, lefts):
    for t in range(NT):
        src, dst, low, high = xs[t], xs[t + 1], t + 1, 10 - t

        def longitude(e, carry, src=src, dst=dst, first=2 * (1 + BASE[t] - low)):
            k = first + 2 * e
            here = [src[var * EXT + e, tile(0)] for var in (0, 1)]
            start = here
            before = [drop(src[var * EXT + e, tile(TILES - 1)], 1) for var in (0, 1)]
            for m in range(TILES):
                c0, up, um, vp, vm = factors(main_c[k, tile(m)], main_c[k + 1, tile(m)])
                after = [src[var * EXT + e, tile(m + 1)] if m < TILES - 1 else drop(start[var], -1) for var in (0, 1)]
                for var in (0, 1):
                    p = var * EXT + e
                    dst[p, tile(m)] = (
                        c0 * here[var]
                        + (up * src[p - 1, tile(m)] + um * src[p + 1, tile(m)])
                        + (vp * before[var] + vm * after[var])
                    )
                before, here = here, after
            return carry

        lax.fori_loop(low, high + 1, longitude, 0)
        for m in range(TILES):
            c0, up, um, vp, vm = factors(left_c[2 * t, tile(m)], left_c[2 * t + 1, tile(m)])
            for var in (0, 1):
                x = lefts[t][var, tile(m)]
                before = lefts[t][var, tile(m - 1)] if m else drop(lefts[t][var, tile(TILES - 1)], 1)
                after = lefts[t][var, tile(m + 1)] if m < TILES - 1 else drop(lefts[t][var, tile(0)], -1)
                lefts[t + 1][var, tile(m)] = (
                    c0 * x + (up * turn(x, REST) + um * turn(x, -REST)) + (vp * before + vm * after)
                )


def adjoint_lats(terms, write):
    stay0, down0, up0 = terms(0)
    last, up_last, first = None, None, None
    pending, rising = stay0, up0
    for m in range(1, TILES):
        stay, down, up = terms(m)
        done = pending + down
        if m == 1:
            first = done
        else:
            write(m - 1, done)
        pending, rising = stay + rising, up
    write(TILES - 1, pending + drop(down0, -1))
    write(0, first + drop(rising, 1))


def adjoint_sweep(main_c, left_c, grads, ys, lefts):
    for t in reversed(range(NT)):
        src, dst, low, high = ys[t + 1], ys[t], t + 1, 10 - t
        for var in (0, 1):
            for l in range(SLAB):
                g = grads[10 * t + 2 * l + var]
                own = var * EXT + SLAB + l
                src[own] = g if t == NT - 1 else src[own] + g
            g = grads[10 * t + 8 + var]
            lefts[t + 1][var] = g if t == NT - 1 else lefts[t + 1][var] + g
            for e in (low - 1, high + 1):
                src[var * EXT + e] = jnp.zeros((ROWS, 128), F32)

        first_plane = 2 * (1 + BASE[t] - low)

        def longitude(e, carry, src=src, dst=dst, first=first_plane):
            k = first + 2 * e
            both = [{}, {}]

            def shared(m):
                if m not in both[0]:
                    from_east = jnp.maximum(main_c[k + 2, tile(m)], 0.0)
                    from_west = jnp.maximum(-main_c[k - 2, tile(m)], 0.0)
                    both[0][m] = (*factors(main_c[k, tile(m)], main_c[k + 1, tile(m)]), from_east, from_west)
                return both[0][m]

            state = [None, None]
            for m in range(TILES):
                c0, _, _, vp, vm, from_east, from_west = shared(m)
                for var in (0, 1):
                    p = var * EXT + e
                    y = src[p, tile(m)]
                    stay = c0 * y + (from_east * src[p + 1, tile(m)] + from_west * src[p - 1, tile(m)])
                    down, up = vp * y, vm * y
                    if m == 0:
                        state[var] = (down, None, stay, up)
                        continue
                    down0, first, pending, rising = state[var]
                    done = pending + down
                    if m == 1:
                        first = done
                    else:
                        dst[p, tile(m - 1)] = done
                    state[var] = (down0, first, stay + rising, up)
            for var in (0, 1):
                down0, first, pending, rising = state[var]
                dst[var * EXT + e, tile(TILES - 1)] = pending + drop(down0, -1)
                dst[var * EXT + e, tile(0)] = first + drop(rising, 1)
            return carry

        lax.fori_loop(low, high + 1, longitude, 0)
        for m in range(TILES):
            west = jnp.maximum(main_c[first_plane + 2 * low, tile(m)], 0.0)
            east = jnp.maximum(-main_c[first_plane + 2 * high, tile(m)], 0.0)
            for var in (0, 1):
                dst[var * EXT + low - 1, tile(m)] = west * src[var * EXT + low, tile(m)]
                dst[var * EXT + high + 1, tile(m)] = east * src[var * EXT + high, tile(m)]
        for var in (0, 1):

            def terms(m, var=var, t=t):
                c0, up, um, vp, vm = factors(left_c[2 * t, tile(m)], left_c[2 * t + 1, tile(m)])
                y = lefts[t + 1][var, tile(m)]
                return c0 * y + (turn(up * y, -REST) + turn(um * y, REST)), vp * y, vm * y

            def write(m, x, var=var, t=t):
                lefts[t][var, tile(m)] = x

            adjoint_lats(terms, write)


def adjoint_outputs(odd, y, left, out_own, out_near, out_far):
    for var in (0, 1):
        for l in range(SLAB):
            k, p = 2 * l + var, var * EXT + l
            west, east = y[p], y[p + 2 * SLAB]
            out_own[k] = y[p + SLAB]
            out_near[k] = jnp.where(odd, west, east)
            out_far[k] = jnp.where(odd, east, west)
        out_own[2 * SLAB + var] = left[var]
    lane = lanes((ROWS, 128))
    west = jnp.where(lane < SHARE, left[0], turn(left[1], SHARE))
    east = jnp.where(lane < SHARE, turn(left[0], -2 * SHARE), turn(left[1], -SHARE))
    out_near[2 * SLAB] = jnp.where(odd, west, east)
    out_far[2 * SLAB] = jnp.where(odd, east, west)


def with_rim(x, m, rim, plane):
    if m < 8:
        return jnp.where(depths() == 0, rim[plane, pl.ds(m, 1)], x)
    if m > 8:
        return jnp.where(depths() == 7, rim[plane, pl.ds(m - 1, 1)], x)
    return x


def inside(m):
    return depths() != (0 if m < 4 else 7 if m >= TILES - 4 else -1)


def halves(x):
    big = x.astype(BF16)
    return big, (x - big.astype(F32)).astype(BF16)


def dot(a, b, across=False):
    dims = (((1,), (1 if across else 0,)), ((), ()))
    return lax.dot_general(a, b, dims, preferred_element_type=F32)


def split_dot(a, b_big, b_small, across=False):
    a_big, a_small = halves(a)
    return dot(a_big, b_big, across) + (dot(a_small, b_big, across) + dot(a_big, b_small, across))


def spread(values, table, others, grads, t):
    main = split_dot(values, *table, True)
    rest = split_dot(jnp.concatenate([values[l * ROWS : (l + 1) * ROWS] for l in range(SLAB)], 1), *others, True)
    for var in (0, 1):
        for l in range(SLAB):
            grads[10 * t + 2 * l + var] = main[l * ROWS : (l + 1) * ROWS, 128 * var : 128 * (var + 1)]
        grads[10 * t + 8 + var] = rest[:, 128 * var : 128 * (var + 1)]


def observe(x, left, table, others):
    rows = [jnp.concatenate([x[SLAB + l], x[EXT + SLAB + l]], 1) for l in range(SLAB)]
    main = split_dot(jnp.concatenate(rows, 0), *table)
    rest = split_dot(jnp.concatenate([left[0], left[1]], 1), *others)
    return main + jnp.concatenate([rest[:, 128 * l : 128 * (l + 1)] for l in range(SLAB)], 0)


def message_kernel(flags, given_weight, given, sent, error_weight, innovations, message, done):
    copies = [
        pltpu.make_async_copy(source, target, done.at[i])
        for i, (source, target) in enumerate(((given_weight, error_weight), (given, innovations)))
    ]
    for copy in copies:
        copy.start()
    for copy in copies:
        copy.wait()
    owners = error_weight.shape[0] // (NT * SLOTS)
    for t in range(NT):
        for c in range(SLOTS):
            here = pl.ds((t * owners) * SLOTS + c, owners, stride=SLOTS)
            weight = error_weight[here]
            message[pl.ds(t * SLOTS + c, owners, stride=2 * NT * SLOTS)] = weight * innovations[here]
            message[pl.ds((NT + t) * SLOTS + c, owners, stride=2 * NT * SLOTS)] = weight
    send = pltpu.make_async_copy(message, sent, done.at[2])
    send.start()
    send.wait()


def prepare_kernel(flags, courant, weighting, own, own_left, to_near, to_far, edges, table, others, lay, mine, packed):
    depth = courant.shape[0] // (2 * NT * SLAB)
    main = depth - REST
    odd = flags[0] == 1
    lay[...] = jnp.zeros(lay.shape, F32)
    mine[...] = jnp.zeros(mine.shape, F32)
    packed[...] = jnp.zeros(packed.shape, F32)

    def place(x, target, plane, edge):
        if edge is not None:
            edges[edge, pl.ds(0, 4)] = x[:4]
            edges[edge, pl.ds(4, 4)] = x[BAND - 4 :]
        lay[pl.ds(4, BAND)] = x
        for m in range(TILES):
            target[plane, tile(m)] = lay[pl.ds(m, 8, stride=TILES)]

    for k in (0, 1):
        for t in range(NT):
            for l in range(SLAB):
                start = (2 * t + k) * depth * SLAB + l
                x = courant[pl.ds(start, main, stride=SLAB)]
                place(x.T, own, 8 * t + 4 * k + l, 2 * (4 * t + l) + k if t < NT - 1 else None)
                x = courant[pl.ds(start + main * SLAB, REST, stride=SLAB)]
                mine[pl.ds((SLAB + l) * REST, REST)] = x
                if t < NT - 1:
                    packed[pl.ds(t * SHARE + l * REST, REST)] = x
            place(mine[...].T, own_left, 2 * t + k, None)
            for d in range(1, NT - t):
                west, east = own[8 * t + 4 * k + d - 1], own[8 * t + 4 * k + SLAB - d]
                to_near[2 * PLANES[t, d] + k] = jnp.where(odd, west, east)
                to_far[2 * PLANES[t, d] + k] = jnp.where(odd, east, west)
        place(packed[...].T, to_near, 12 + k, 24 + k)
        to_far[12 + k] = to_near[12 + k]
    others[...] = jnp.zeros(others.shape, F32)
    for var in (0, 1):
        table[pl.ds(128 * var, main)] = weighting[pl.ds(depth * var, main)]
        rest = weighting[pl.ds(depth * var + main, REST)]
        for l in range(SLAB):
            others[pl.ds(128 * var + (SLAB + l) * REST, REST), pl.ds(128 * l, 128)] = rest


def halo_kernel(flags, south, north, halo):
    row = lax.broadcasted_iota(jnp.int32, south.shape[1:], 0)
    for k in range(south.shape[0]):
        below = jnp.where(flags[1] > 0, drop(south[k], 4), 0.0)
        above = jnp.where(flags[1] < flags[2] - 1, drop(north[k], 4), 0.0)
        halo[k] = jnp.where(row < 4, below, above)


def complete(flags, mine, south, north, k):
    has_south, has_north = flags[1] > 0, flags[1] < flags[2] - 1
    low = jnp.where(has_south, south[k, pl.ds(8, 8)], 0.0) + mine[k, pl.ds(0, 8)]
    high = jnp.where(has_north, north[k, pl.ds(0, 8)], 0.0) + mine[k, pl.ds(8, 8)]
    row = depths()
    return (
        jnp.where(row < 4, jnp.where(has_south, low, 0.0), low),
        jnp.where(row < 4, high, jnp.where(has_north, high, 0.0)),
    )


def edge_kernel(flags, mine, south, north, edge):
    for k in range(edge.shape[0]):
        low, high = complete(flags, mine, south, north, k)
        edge[k, pl.ds(0, 8)] = low
        edge[k, pl.ds(8, 8)] = high


def slots_kernel(flags, sent, index, counts, table, others, weights, grads):
    table, others = halves(table[...]), halves(others[...])
    owners = counts.shape[1]
    shape = (SLAB, TILES, 8, owners)
    l, m, s = (lax.broadcasted_iota(jnp.int32, shape, axis) for axis in range(3))
    latitude = TILES * s + m - 4
    cell = jnp.where((latitude >= 0) & (latitude < BAND), l * BAND + latitude, -2).reshape(SLAB * ROWS, owners)
    for t in range(NT):
        hits, bigs, smalls = [], [], []
        for c in range(SLOTS):
            slot = jnp.where(c < counts[pl.ds(t, 1), :], index[t, pl.ds(c, 1), :], -1)
            hits.append(jnp.where(cell == slot, 1.0, 0.0).astype(BF16))
            both = [sent[pl.ds((i * NT + t) * SLOTS + c, owners, stride=2 * NT * SLOTS)] for i in (0, 1)]
            big, small = halves(jnp.concatenate(both, 1))
            bigs.append(big)
            smalls.append(small)
        hit = jnp.concatenate(hits, 1)
        total = dot(hit, jnp.concatenate(bigs, 0)) + dot(hit, jnp.concatenate(smalls, 0))
        weights[t] = total[:, 128:]
        spread(total[:, :128], table, others, grads, t)


def right_side_kernel(flags, grads, own, own_left, packed, near, far, halo, halo_near, halo_far, *rest):
    out_own, out_near, out_far, main_c, left_c, whole, *scratch = rest
    odd = flags[0] == 1
    lane, row = lanes(), depths()

    def tiles(target, plane, tile_of, halo_of):
        for m in range(TILES):
            x = tile_of(m)
            if halo_of is not None and m < 4:
                x = jnp.where(row == 0, halo_of(m), x)
            if halo_of is not None and m >= TILES - 4:
                x = jnp.where(row == 7, halo_of(m - (TILES - 8)), x)
            target[plane, tile(m)] = x

    for k in (0, 1):
        main_c[k] = jnp.zeros((ROWS, 128), F32)
        main_c[58 + k] = jnp.zeros((ROWS, 128), F32)
        for t in range(NT):
            for e in range(t + 1, 11 - t):
                plane = 2 * (1 + BASE[t] + e - t - 1) + k
                strip = 2 * (4 * t + e % SLAB) + k
                if SLAB <= e < 2 * SLAB:
                    source = 8 * t + 4 * k + e - SLAB
                    tiles(
                        main_c, plane, lambda m, p=source: own[p, tile(m)],
                        (lambda i, p=strip: halo[p, pl.ds(i, 1)]) if t < NT - 1 else None,
                    )
                    continue
                source = 2 * PLANES[t, SLAB - e if e < SLAB else e - 2 * SLAB + 1] + k
                a, b, ha, hb = (near, far, halo_near, halo_far) if e < SLAB else (far, near, halo_far, halo_near)
                tiles(
                    main_c, plane,
                    lambda m, p=source, a=a, b=b: jnp.where(odd, a[p, tile(m)], b[p, tile(m)]),
                    lambda i, p=strip, a=ha, b=hb: jnp.where(odd, a[p, pl.ds(i, 1)], b[p, pl.ds(i, 1)]),
                )
        tiles(whole, 0, lambda m: packed[k, tile(m)], lambda i: halo[24 + k, pl.ds(i, 1)])
        for part, (a, b, ha, hb) in ((1, (near, far, halo_near, halo_far)), (2, (far, near, halo_far, halo_near))):
            tiles(
                whole, part,
                lambda m, a=a, b=b: jnp.where(odd, a[12 + k, tile(m)], b[12 + k, tile(m)]),
                lambda i, a=ha, b=hb: jnp.where(odd, a[24 + k, pl.ds(i, 1)], b[24 + k, pl.ds(i, 1)]),
            )
        for t in range(NT):
            for m in range(TILES):
                if t == NT - 1:
                    left_c[2 * t + k, tile(m)] = own_left[2 * t + k, tile(m)]
                    continue
                mid, west, east = (whole[i, tile(m)] for i in range(3))
                x = jnp.where(lane < SHARE, turn(west, -SHARE * t), turn(mid, SHARE - SHARE * t))
                x = jnp.where(lane < 2 * SHARE, x, turn(east, 2 * SHARE - SHARE * t))
                left_c[2 * t + k, tile(m)] = jnp.where(lane < 3 * SHARE, x, 0.0)
    ys, lefts = scratch[: NT + 1], scratch[NT + 1 :]
    adjoint_sweep(main_c, left_c, grads, ys, lefts)
    adjoint_outputs(odd, ys[0], lefts[0], out_own, out_near, out_far)


def hessian_kernel(flags, own, near, far, e_own, e_near, e_far, weights, table, others, moments, main_c, left_c, *rest):
    out_own, out_near, out_far, out_field, out_moments, grads, *scratch = rest
    xs, lefts = scratch[: NT + 1], scratch[NT + 1 :]
    odd = flags[0] == 1
    lane = lanes()
    square = jnp.zeros((8, 128), F32)
    for m in range(TILES):
        for k in range(2 * SLAB + 1):
            a = with_rim(own[k, tile(m)], m, e_own, k)
            b = with_rim(near[k, tile(m)], m, e_near, k)
            c = with_rim(far[k, tile(m)], m, e_far, k)
            west, east = jnp.where(odd, b, c), jnp.where(odd, c, b)
            out_field[k, tile(m)] = a
            counted = inside(m)
            if k < 2 * SLAB:
                p = (k % 2) * EXT + k // 2
                for i, x in enumerate((west, a, east)):
                    xs[0][p + SLAB * i, tile(m)] = x
            else:
                counted = counted & (lane >= SHARE) & (lane < 3 * SHARE)
                for var in (0, 1):
                    x = jnp.where(lane < SHARE, turn(west, -SHARE * (1 + var)), turn(a, -SHARE * var))
                    x = jnp.where(lane < 2 * SHARE, x, turn(east, SHARE - SHARE * var))
                    lefts[0][var, tile(m)] = jnp.where(lane < 3 * SHARE, x, 0.0)
            square = square + jnp.where(counted, a * a, 0.0)
    forward_sweep(main_c, left_c, xs, lefts)
    table, others = halves(table[...]), halves(others[...])
    product = jnp.zeros((8, 128), F32)
    for t in range(NT):
        seen = observe(xs[t + 1], lefts[t + 1], table, others)
        weighed = weights[t] * seen
        product = product + jnp.sum((weighed * seen).reshape(-1, 8, 128), axis=0)
        spread(weighed, table, others, grads, t)
    lane = lanes(out_moments.shape)
    before = moments[pl.ds(0, 1), :]
    found = jnp.where(lane == 2, jnp.sum(square), jnp.where(lane == 3, jnp.sum(product), 0.0))
    out_moments[...] = jnp.where(lane < 2, turn(jnp.broadcast_to(before, lane.shape), -2), found)
    adjoint_sweep(main_c, left_c, grads, xs, lefts)
    adjoint_outputs(odd, xs[0], lefts[0], out_own, out_near, out_far)


def gather_kernel(flags, own, near, far, *rest):
    main, rim = rest[-2:]
    lane = lanes()
    for k in range(2 * SLAB + 1):
        for m in range(TILES):
            if k < 2 * SLAB:
                x = own[k, tile(m)] + (near[k, tile(m)] + far[k, tile(m)])
            else:
                more = near[k, tile(m)] + far[k, tile(m)]
                first = own[k, tile(m)] + turn(more, SHARE)
                second = own[k + 1, tile(m)] + more
                x = jnp.where(lane < 2 * SHARE, first, turn(second, SHARE))
                x = jnp.where((lane >= SHARE) & (lane < 3 * SHARE), x, 0.0)
            main[k, tile(m)] = x
        for m in range(8):
            rim[k, pl.ds(m, 1)] = main[k, pl.ds(8 * m, 1)]
            rim[k, pl.ds(m + 8, 1)] = main[k, pl.ds(8 * (m + 9) + 7, 1)]


def final_kernel(flags, v0, v1, main, mine, south, north, sums, solution, residual, edge, lay_s, lay_r):
    total = jnp.sum(sums[...], axis=0, keepdims=True)
    lane = lanes(total.shape)
    m = [jnp.sum(jnp.where(lane == k, total, 0.0), axis=1, keepdims=True) for k in range(4)]
    a, c, d = m[1] / m[0], m[2] / m[0], m[3] / m[0]
    step0 = 1.0 / (1.0 + a)
    keep = a * step0
    ratio = (c - a * a) * step0 * step0
    p, s = keep + ratio, -step0
    curvature = p * p + 2.0 * p * s * a + s * s * c + (p * p * a + 2.0 * p * s * c + s * s * d)
    step1 = ratio / curvature
    for_s = (step0 + step1 * p, step1 * s)
    for_r = (keep - step1 * p, s - step1 * (p + s), -(step1 * s))
    depth = solution.shape[0] // (2 * SLAB)
    edge_kernel(flags, mine, south, north, edge)
    for k in range(2 * SLAB + 1):
        for m in range(TILES):
            x0, x1 = v0[k, tile(m)], v1[k, tile(m)]
            x2 = with_rim(main[k, tile(m)], m, edge, k)
            lay_s[pl.ds(m, 8, stride=TILES)] = for_s[0] * x0 + for_s[1] * x1
            lay_r[pl.ds(m, 8, stride=TILES)] = for_r[0] * x0 + for_r[1] * x1 + for_r[2] * x2
        for lay, out in ((lay_s, solution), (lay_r, residual)):
            x = lay[pl.ds(4, BAND)].T
            if k < 2 * SLAB:
                out[pl.ds((k % 2) * depth * SLAB + k // 2, 128, stride=SLAB)] = x
                continue
            for var in (0, 1):
                for l in range(SLAB):
                    row = SHARE * (1 + var) + REST * l
                    out[pl.ds((var * depth + 128) * SLAB + l, REST, stride=SLAB)] = x[row : row + REST]


def shift(x, axis, by):
    n = lax.axis_size(axis)
    return lax.ppermute(x, axis, [(i, (i + by) % n) for i in range(n)])


def far_swap(x):
    n = lax.axis_size("lon")
    return lax.ppermute(x, "lon", [(i, (i + 1 if i % 2 else i - 1) % n) for i in range(n)])


def near_swap(x):
    return lax.ppermute(x, "lon", [(i, i ^ 1) for i in range(lax.axis_size("lon"))])


def body(courant, slot_column_cells, column_counts, innovations, error_weight, weighting):
    depth = courant.shape[2]
    owners = slot_column_cells.shape[2]
    channels = weighting.shape[1]
    flags = jnp.stack([lax.axis_index("lon") % 2, lax.axis_index("lat"), jnp.int32(lax.axis_size("lat"))]).astype(jnp.int32)
    slots = owners * SLOTS

    (message,) = call(
        message_kernel,
        [(2 * NT * slots, channels)],
        [flags, error_weight.reshape(NT * slots, channels), innovations.reshape(NT * slots, channels)],
        [
            pltpu.VMEM((NT * slots, channels), F32), pltpu.VMEM((NT * slots, channels), F32),
            pltpu.VMEM((2 * NT * slots, channels), F32), pltpu.SemaphoreType.DMA((3,)),
        ],
        hbm_in=(1, 2),
        hbm_out=(0,),
    )
    sent = lax.all_to_all(
        message.reshape(owners, 2 * NT * SLOTS, channels), ("lon", "lat"), split_axis=0, concat_axis=0, tiled=True
    ).reshape(2 * NT * slots, channels)
    own, own_left, to_near, to_far, edges, table, others = call(
        prepare_kernel,
        [
            (2 * NT * SLAB, ROWS, 128), (2 * NT, ROWS, 128), (14, ROWS, 128), (14, ROWS, 128), (26, 8, 128),
            (256, channels), (256, SLAB * channels),
        ],
        [flags, courant.reshape(2 * NT * depth * SLAB, BAND), weighting],
        [pltpu.VMEM((ROWS, 128), F32), pltpu.VMEM((128, 128), F32), pltpu.VMEM((128, 128), F32)],
    )
    c_far, c_near = far_swap(to_far), near_swap(to_near)
    (halo,) = call(halo_kernel, [(26, 8, 128)], [flags, shift(edges, "lat", 1), shift(edges, "lat", -1)])
    index = jnp.swapaxes(slot_column_cells[:, 0], 1, 2)

    parcel = (2 * SLAB + 1, ROWS, 128)
    rim = (2 * SLAB + 1, 16, 128)
    pieces = [(2 * SLAB + 2, ROWS, 128), parcel, parcel]
    steps = [pltpu.VMEM((2 * EXT, ROWS, 128), F32)] * (NT + 1) + [pltpu.VMEM((2, ROWS, 128), F32)] * (NT + 1)

    def gathered(parts, *more):
        mine, to_near, to_far = parts
        return call(gather_kernel, [parcel, rim], [flags, mine, near_swap(to_near), far_swap(to_far), *more])

    def hessian(state, moments, rows):
        main, mine = state
        (edge,) = call(edge_kernel, [rim], [flags, mine, shift(mine, "lat", 1), shift(mine, "lat", -1)])
        return call(
            hessian_kernel,
            [*pieces, parcel, (rows, 128)],
            [
                flags, main, near_swap(main), far_swap(main), edge, near_swap(edge), far_swap(edge),
                weights, table, others, moments, main_c, left_c,
            ],
            [pltpu.VMEM((10 * NT, ROWS, 128), F32), *steps],
        )

    weights, right = call(
        slots_kernel,
        [(NT, SLAB * ROWS, channels), (10 * NT, ROWS, 128)],
        [flags, sent, index, column_counts[:, 0], table, others],
    )
    *parts, main_c, left_c = call(
        right_side_kernel,
        [*pieces, (60, ROWS, 128), (2 * NT, ROWS, 128)],
        [flags, right, own, own_left, to_near[12:], c_near, c_far, halo, near_swap(halo), far_swap(halo)],
        [pltpu.VMEM((3, ROWS, 128), F32), *steps],
    )
    *parts, v0, moments = hessian(gathered(parts), jnp.zeros((8, 128), F32), 8)
    *parts, v1, moments = hessian(gathered(parts), moments, owners)
    sums = lax.all_to_all(moments, ("lon", "lat"), split_axis=0, concat_axis=0, tiled=True)
    main, mine = gathered(parts, sums)
    solution, residual = call(
        final_kernel,
        [(2 * depth * SLAB, BAND)] * 2,
        [flags, v0, v1, main, mine, shift(mine, "lat", 1), shift(mine, "lat", -1), sums],
        [pltpu.VMEM(rim, F32), pltpu.VMEM((ROWS, 128), F32), pltpu.VMEM((ROWS, 128), F32)],
    )
    shape = (2, depth, SLAB, BAND)
    return solution.reshape(shape), residual.reshape(shape)


def solution(mesh):
    in_specs = (
        P(None, None, None, "lon", "lat"),
        P(None, ("lon", "lat"), None, None),
        P(None, ("lon", "lat"), None),
        P(None, ("lon", "lat"), None, None, None),
        P(None, ("lon", "lat"), None, None, None),
        P(),
    )
    out_specs = (P(None, None, "lon", "lat"), P(None, None, "lon", "lat"))
    return jax.shard_map(body, mesh=mesh, in_specs=in_specs, out_specs=out_specs, check_vma=False)
```

```python
import functools

import jax
import jax.numpy as jnp
from jax import lax
from jax.experimental import pallas as pl
from jax.experimental.pallas import tpu as pltpu
from jax.sharding import PartitionSpec as P

F32 = jnp.float32
BF16 = jnp.bfloat16
NT = 4
SLAB = 4
BAND = 128
EXT = 3 * SLAB
SLOTS = 4
TILES = 17
ROWS = 8 * TILES
REST = 9
SHARE = SLAB * REST
BASE = (0, 10, 18, 24)
PLANES = {(0, 1): 0, (0, 2): 1, (0, 3): 2, (1, 1): 3, (1, 2): 4, (2, 1): 5}
VMEM = pl.BlockSpec(memory_space=pltpu.VMEM)


def call(kernel, shapes, inputs, scratch=(), flops=0):
    nbytes = sum(x.size * x.dtype.itemsize for x in inputs)
    return pl.pallas_call(
        kernel,
        out_shape=[jax.ShapeDtypeStruct(s, F32) for s in shapes],
        in_specs=[VMEM] * len(inputs),
        out_specs=[VMEM] * len(shapes),
        scratch_shapes=list(scratch),
        compiler_params=pltpu.CompilerParams(vmem_limit_bytes=32 << 20),
        cost_estimate=pl.CostEstimate(flops=flops, bytes_accessed=nbytes, transcendentals=0),
    )(*inputs)


def turn(x, shift):
    shift %= 128
    return pltpu.roll(x, shift, 1) if shift else x


def is_odd():
    return lax.rem(lax.axis_index("lon"), 2) == 1


def has_bands():
    band = lax.axis_index("lat")
    return band > 0, band < lax.axis_size("lat") - 1


def drop(x, by):
    return pltpu.roll(x, by % 8, 0)


def lanes(shape=(8, 128)):
    return lax.broadcasted_iota(jnp.int32, shape, len(shape) - 1)


def depths():
    return lax.broadcasted_iota(jnp.int32, (8, 128), 0)


def tile(m):
    return pl.ds(8 * m, 8)


def parts(u):
    plus = jnp.maximum(u, 0.0)
    return plus, plus - u


def factors(u, v):
    up, um = parts(u)
    vp, vm = parts(v)
    return 1.0 - (up + um) - (vp + vm), up, um, vp, vm


def forward_sweep(main_c, left_c, xs, lefts):
    for t in range(NT):
        src, dst, low, high = xs[t], xs[t + 1], t + 1, 10 - t

        def longitude(e, carry, src=src, dst=dst, first=2 * (1 + BASE[t] - low)):
            k = first + 2 * e
            here = [src[var * EXT + e, tile(0)] for var in (0, 1)]
            start = here
            before = [drop(src[var * EXT + e, tile(TILES - 1)], 1) for var in (0, 1)]
            for m in range(TILES):
                c0, up, um, vp, vm = factors(main_c[k, tile(m)], main_c[k + 1, tile(m)])
                after = [src[var * EXT + e, tile(m + 1)] if m < TILES - 1 else drop(start[var], -1) for var in (0, 1)]
                for var in (0, 1):
                    p = var * EXT + e
                    dst[p, tile(m)] = (
                        c0 * here[var]
                        + (up * src[p - 1, tile(m)] + um * src[p + 1, tile(m)])
                        + (vp * before[var] + vm * after[var])
                    )
                before, here = here, after
            return carry

        lax.fori_loop(low, high + 1, longitude, 0)
        for m in range(TILES):
            c0, up, um, vp, vm = factors(left_c[2 * t, tile(m)], left_c[2 * t + 1, tile(m)])
            for var in (0, 1):
                x = lefts[t][var, tile(m)]
                before = lefts[t][var, tile(m - 1)] if m else drop(lefts[t][var, tile(TILES - 1)], 1)
                after = lefts[t][var, tile(m + 1)] if m < TILES - 1 else drop(lefts[t][var, tile(0)], -1)
                lefts[t + 1][var, tile(m)] = (
                    c0 * x + (up * turn(x, REST) + um * turn(x, -REST)) + (vp * before + vm * after)
                )


def adjoint_lats(terms, write):
    stay0, down0, up0 = terms(0)
    last, up_last, first = None, None, None
    pending, rising = stay0, up0
    for m in range(1, TILES):
        stay, down, up = terms(m)
        done = pending + down
        if m == 1:
            first = done
        else:
            write(m - 1, done)
        pending, rising = stay + rising, up
    write(TILES - 1, pending + drop(down0, -1))
    write(0, first + drop(rising, 1))


def adjoint_sweep(main_c, left_c, grads, ys, lefts):
    for t in reversed(range(NT)):
        src, dst, low, high = ys[t + 1], ys[t], t + 1, 10 - t
        for var in (0, 1):
            for l in range(SLAB):
                g = grads[10 * t + 2 * l + var]
                own = var * EXT + SLAB + l
                src[own] = g if t == NT - 1 else src[own] + g
            g = grads[10 * t + 8 + var]
            lefts[t + 1][var] = g if t == NT - 1 else lefts[t + 1][var] + g
            for e in (low - 1, high + 1):
                src[var * EXT + e] = jnp.zeros((ROWS, 128), F32)

        first_plane = 2 * (1 + BASE[t] - low)

        def longitude(e, carry, src=src, dst=dst, first=first_plane):
            k = first + 2 * e
            both = [{}, {}]

            def shared(m):
                if m not in both[0]:
                    from_east = jnp.maximum(main_c[k + 2, tile(m)], 0.0)
                    from_west = jnp.maximum(-main_c[k - 2, tile(m)], 0.0)
                    both[0][m] = (*factors(main_c[k, tile(m)], main_c[k + 1, tile(m)]), from_east, from_west)
                return both[0][m]

            state = [None, None]
            for m in range(TILES):
                c0, _, _, vp, vm, from_east, from_west = shared(m)
                for var in (0, 1):
                    p = var * EXT + e
                    y = src[p, tile(m)]
                    stay = c0 * y + (from_east * src[p + 1, tile(m)] + from_west * src[p - 1, tile(m)])
                    down, up = vp * y, vm * y
                    if m == 0:
                        state[var] = (down, None, stay, up)
                        continue
                    down0, first, pending, rising = state[var]
                    done = pending + down
                    if m == 1:
                        first = done
                    else:
                        dst[p, tile(m - 1)] = done
                    state[var] = (down0, first, stay + rising, up)
            for var in (0, 1):
                down0, first, pending, rising = state[var]
                dst[var * EXT + e, tile(TILES - 1)] = pending + drop(down0, -1)
                dst[var * EXT + e, tile(0)] = first + drop(rising, 1)
            return carry

        lax.fori_loop(low, high + 1, longitude, 0)
        for m in range(TILES):
            west = jnp.maximum(main_c[first_plane + 2 * low, tile(m)], 0.0)
            east = jnp.maximum(-main_c[first_plane + 2 * high, tile(m)], 0.0)
            for var in (0, 1):
                dst[var * EXT + low - 1, tile(m)] = west * src[var * EXT + low, tile(m)]
                dst[var * EXT + high + 1, tile(m)] = east * src[var * EXT + high, tile(m)]
        for var in (0, 1):

            def terms(m, var=var, t=t):
                c0, up, um, vp, vm = factors(left_c[2 * t, tile(m)], left_c[2 * t + 1, tile(m)])
                y = lefts[t + 1][var, tile(m)]
                return c0 * y + (turn(up * y, -REST) + turn(um * y, REST)), vp * y, vm * y

            def write(m, x, var=var, t=t):
                lefts[t][var, tile(m)] = x

            adjoint_lats(terms, write)


def adjoint_outputs(odd, y, left, out_own, out_near, out_far):
    for var in (0, 1):
        for l in range(SLAB):
            k, p = 2 * l + var, var * EXT + l
            west, east = y[p], y[p + 2 * SLAB]
            out_own[k] = y[p + SLAB]
            out_near[k] = jnp.where(odd, west, east)
            out_far[k] = jnp.where(odd, east, west)
        out_own[2 * SLAB + var] = left[var]
    lane = lanes((ROWS, 128))
    west = jnp.where(lane < SHARE, left[0], turn(left[1], SHARE))
    east = jnp.where(lane < SHARE, turn(left[0], -2 * SHARE), turn(left[1], -SHARE))
    out_near[2 * SLAB] = jnp.where(odd, west, east)
    out_far[2 * SLAB] = jnp.where(odd, east, west)


def with_rim(x, m, rim, plane):
    if m < 8:
        return jnp.where(depths() == 0, rim[plane, pl.ds(m, 1)], x)
    if m > 8:
        return jnp.where(depths() == 7, rim[plane, pl.ds(m - 1, 1)], x)
    return x


def inside(m):
    return depths() != (0 if m < 4 else 7 if m >= TILES - 4 else -1)


def halves(x):
    big = x.astype(BF16)
    return big, (x - big.astype(F32)).astype(BF16)


def dot(a, b, across=False):
    dims = (((1,), (1 if across else 0,)), ((), ()))
    return lax.dot_general(a, b, dims, preferred_element_type=F32)


def split_dot(a, b_big, b_small, across=False):
    a_big, a_small = halves(a)
    return dot(a_big, b_big, across) + (dot(a_small, b_big, across) + dot(a_big, b_small, across))


def spread(values, table, others, grads, t):
    main = split_dot(values, *table, True)
    rest = split_dot(jnp.concatenate([values[l * ROWS : (l + 1) * ROWS] for l in range(SLAB)], 1), *others, True)
    for var in (0, 1):
        for l in range(SLAB):
            grads[10 * t + 2 * l + var] = main[l * ROWS : (l + 1) * ROWS, 128 * var : 128 * (var + 1)]
        grads[10 * t + 8 + var] = rest[:, 128 * var : 128 * (var + 1)]


def observe(x, left, table, others):
    rows = [jnp.concatenate([x[SLAB + l], x[EXT + SLAB + l]], 1) for l in range(SLAB)]
    main = split_dot(jnp.concatenate(rows, 0), *table)
    rest = split_dot(jnp.concatenate([left[0], left[1]], 1), *others)
    return main + jnp.concatenate([rest[:, 128 * l : 128 * (l + 1)] for l in range(SLAB)], 0)


def prepare_kernel(courant, weighting, own, own_left, out_packed, to_near, to_far, edges, table, others, *scratch):
    lay, mine, packed = scratch
    depth = courant.shape[0] // (2 * NT * SLAB)
    main = depth - REST
    odd = is_odd()
    lay[...] = jnp.zeros(lay.shape, F32)
    mine[...] = jnp.zeros(mine.shape, F32)
    packed[...] = jnp.zeros(packed.shape, F32)

    def place(x, target, plane, edge):
        if edge is not None:
            edges[edge, pl.ds(0, 4)] = x[:4]
            edges[edge, pl.ds(4, 4)] = x[BAND - 4 :]
        lay[pl.ds(4, BAND)] = x
        for m in range(TILES):
            target[plane, tile(m)] = lay[pl.ds(m, 8, stride=TILES)]

    for k in (0, 1):
        for t in range(NT):
            for l in range(SLAB):
                start = (2 * t + k) * depth * SLAB + l
                x = courant[pl.ds(start, main, stride=SLAB)]
                place(x.T, own, 8 * t + 4 * k + l, 2 * (4 * t + l) + k if t < NT - 1 else None)
                x = courant[pl.ds(start + main * SLAB, REST, stride=SLAB)]
                mine[pl.ds((SLAB + l) * REST, REST)] = x
                if t < NT - 1:
                    packed[pl.ds(t * SHARE + l * REST, REST)] = x
            place(mine[...].T, own_left, 2 * t + k, None)
            for d in range(1, NT - t):
                west, east = own[8 * t + 4 * k + d - 1], own[8 * t + 4 * k + SLAB - d]
                to_near[2 * PLANES[t, d] + k] = jnp.where(odd, west, east)
                to_far[2 * PLANES[t, d] + k] = jnp.where(odd, east, west)
        place(packed[...].T, out_packed, k, 24 + k)
        to_near[12 + k] = out_packed[k]
        to_far[12 + k] = out_packed[k]
    others[...] = jnp.zeros(others.shape, F32)
    for var in (0, 1):
        table[pl.ds(128 * var, main)] = weighting[pl.ds(depth * var, main)]
        rest = weighting[pl.ds(depth * var + main, REST)]
        for l in range(SLAB):
            others[pl.ds(128 * var + (SLAB + l) * REST, REST), pl.ds(128 * l, 128)] = rest


def halo_kernel(south, north, halo):
    row = depths()
    has_south, has_north = has_bands()
    for k in range(south.shape[0]):
        below = jnp.where(has_south, drop(south[k], 4), 0.0)
        above = jnp.where(has_north, drop(north[k], 4), 0.0)
        halo[k] = jnp.where(row < 4, below, above)


def complete(mine, south, north, k):
    has_south, has_north = has_bands()
    low = jnp.where(has_south, south[k, pl.ds(8, 8)], 0.0) + mine[k, pl.ds(0, 8)]
    high = jnp.where(has_north, north[k, pl.ds(0, 8)], 0.0) + mine[k, pl.ds(8, 8)]
    row = depths()
    return (
        jnp.where(row < 4, jnp.where(has_south, low, 0.0), low),
        jnp.where(row < 4, high, jnp.where(has_north, high, 0.0)),
    )


def edge_kernel(mine, south, north, edge):
    for k in range(edge.shape[0]):
        low, high = complete(mine, south, north, k)
        edge[k, pl.ds(0, 8)] = low
        edge[k, pl.ds(8, 8)] = high


def slots_kernel(sent, index, counts, table, others, weights, grads):
    table, others = halves(table[...]), halves(others[...])
    owners = counts.shape[1]
    shape = (SLAB, TILES, 8, owners)
    l, m, s = (lax.broadcasted_iota(jnp.int32, shape, axis) for axis in range(3))
    latitude = TILES * s + m - 4
    cell = jnp.where((latitude >= 0) & (latitude < BAND), l * BAND + latitude, -2).reshape(SLAB * ROWS, owners)
    for t in range(NT):
        hits, bigs, smalls = [], [], []
        for c in range(SLOTS):
            slot = jnp.where(c < counts[pl.ds(t, 1), :], index[t, pl.ds(c, 1), :], -1)
            hits.append(jnp.where(cell == slot, 1.0, 0.0).astype(BF16))
            both = [sent[pl.ds((i * NT + t) * SLOTS + c, owners, stride=2 * NT * SLOTS)] for i in (0, 1)]
            big, small = halves(jnp.concatenate(both, 1))
            bigs.append(big)
            smalls.append(small)
        hit = jnp.concatenate(hits, 1)
        total = dot(hit, jnp.concatenate(bigs, 0)) + dot(hit, jnp.concatenate(smalls, 0))
        weights[t] = total[:, 128:]
        spread(total[:, :128], table, others, grads, t)


def right_side_kernel(grads, own, own_left, packed, near, far, halo, halo_near, halo_far, *rest):
    out_own, out_near, out_far, main_c, left_c, whole, *scratch = rest
    odd = is_odd()
    lane, row = lanes(), depths()

    def tiles(target, plane, tile_of, halo_of):
        for m in range(TILES):
            x = tile_of(m)
            if halo_of is not None and m < 4:
                x = jnp.where(row == 0, halo_of(m), x)
            if halo_of is not None and m >= TILES - 4:
                x = jnp.where(row == 7, halo_of(m - (TILES - 8)), x)
            target[plane, tile(m)] = x

    for k in (0, 1):
        main_c[k] = jnp.zeros((ROWS, 128), F32)
        main_c[58 + k] = jnp.zeros((ROWS, 128), F32)
        for t in range(NT):
            for e in range(t + 1, 11 - t):
                plane = 2 * (1 + BASE[t] + e - t - 1) + k
                strip = 2 * (4 * t + e % SLAB) + k
                if SLAB <= e < 2 * SLAB:
                    source = 8 * t + 4 * k + e - SLAB
                    tiles(
                        main_c, plane, lambda m, p=source: own[p, tile(m)],
                        (lambda i, p=strip: halo[p, pl.ds(i, 1)]) if t < NT - 1 else None,
                    )
                    continue
                source = 2 * PLANES[t, SLAB - e if e < SLAB else e - 2 * SLAB + 1] + k
                a, b, ha, hb = (near, far, halo_near, halo_far) if e < SLAB else (far, near, halo_far, halo_near)
                tiles(
                    main_c, plane,
                    lambda m, p=source, a=a, b=b: jnp.where(odd, a[p, tile(m)], b[p, tile(m)]),
                    lambda i, p=strip, a=ha, b=hb: jnp.where(odd, a[p, pl.ds(i, 1)], b[p, pl.ds(i, 1)]),
                )
        tiles(whole, 0, lambda m: packed[k, tile(m)], lambda i: halo[24 + k, pl.ds(i, 1)])
        for part, (a, b, ha, hb) in ((1, (near, far, halo_near, halo_far)), (2, (far, near, halo_far, halo_near))):
            tiles(
                whole, part,
                lambda m, a=a, b=b: jnp.where(odd, a[12 + k, tile(m)], b[12 + k, tile(m)]),
                lambda i, a=ha, b=hb: jnp.where(odd, a[24 + k, pl.ds(i, 1)], b[24 + k, pl.ds(i, 1)]),
            )
        for t in range(NT):
            for m in range(TILES):
                if t == NT - 1:
                    left_c[2 * t + k, tile(m)] = own_left[2 * t + k, tile(m)]
                    continue
                mid, west, east = (whole[i, tile(m)] for i in range(3))
                x = jnp.where(lane < SHARE, turn(west, -SHARE * t), turn(mid, SHARE - SHARE * t))
                x = jnp.where(lane < 2 * SHARE, x, turn(east, 2 * SHARE - SHARE * t))
                left_c[2 * t + k, tile(m)] = jnp.where(lane < 3 * SHARE, x, 0.0)
    ys, lefts = scratch[: NT + 1], scratch[NT + 1 :]
    adjoint_sweep(main_c, left_c, grads, ys, lefts)
    adjoint_outputs(odd, ys[0], lefts[0], out_own, out_near, out_far)


def hessian_kernel(own, near, far, e_own, e_near, e_far, weights, table, others, moments, main_c, left_c, *rest):
    out_own, out_near, out_far, out_field, out_moments, grads, *scratch = rest
    xs, lefts = scratch[: NT + 1], scratch[NT + 1 :]
    odd = is_odd()
    lane = lanes()
    square = jnp.zeros((8, 128), F32)
    for m in range(TILES):
        for k in range(2 * SLAB + 1):
            a = with_rim(own[k, tile(m)], m, e_own, k)
            b = with_rim(near[k, tile(m)], m, e_near, k)
            c = with_rim(far[k, tile(m)], m, e_far, k)
            west, east = jnp.where(odd, b, c), jnp.where(odd, c, b)
            out_field[k, tile(m)] = a
            counted = inside(m)
            if k < 2 * SLAB:
                p = (k % 2) * EXT + k // 2
                for i, x in enumerate((west, a, east)):
                    xs[0][p + SLAB * i, tile(m)] = x
            else:
                counted = counted & (lane >= SHARE) & (lane < 3 * SHARE)
                for var in (0, 1):
                    x = jnp.where(lane < SHARE, turn(west, -SHARE * (1 + var)), turn(a, -SHARE * var))
                    x = jnp.where(lane < 2 * SHARE, x, turn(east, SHARE - SHARE * var))
                    lefts[0][var, tile(m)] = jnp.where(lane < 3 * SHARE, x, 0.0)
            square = square + jnp.where(counted, a * a, 0.0)
    forward_sweep(main_c, left_c, xs, lefts)
    table, others = halves(table[...]), halves(others[...])
    product = jnp.zeros((8, 128), F32)
    for t in range(NT):
        seen = observe(xs[t + 1], lefts[t + 1], table, others)
        weighed = weights[t] * seen
        product = product + jnp.sum((weighed * seen).reshape(-1, 8, 128), axis=0)
        spread(weighed, table, others, grads, t)
    lane = lanes(out_moments.shape)
    before = moments[pl.ds(0, 1), :]
    found = jnp.where(lane == 2, jnp.sum(square), jnp.where(lane == 3, jnp.sum(product), 0.0))
    out_moments[...] = jnp.where(lane < 2, turn(jnp.broadcast_to(before, lane.shape), -2), found)
    adjoint_sweep(main_c, left_c, grads, xs, lefts)
    adjoint_outputs(odd, xs[0], lefts[0], out_own, out_near, out_far)


def gather_kernel(own, near, far, *rest):
    main, rim = rest[-2:]
    lane = lanes()
    for k in range(2 * SLAB + 1):
        for m in range(TILES):
            if k < 2 * SLAB:
                x = own[k, tile(m)] + (near[k, tile(m)] + far[k, tile(m)])
            else:
                more = near[k, tile(m)] + far[k, tile(m)]
                first = own[k, tile(m)] + turn(more, SHARE)
                second = own[k + 1, tile(m)] + more
                x = jnp.where(lane < 2 * SHARE, first, turn(second, SHARE))
                x = jnp.where((lane >= SHARE) & (lane < 3 * SHARE), x, 0.0)
            main[k, tile(m)] = x
        for m in range(8):
            rim[k, pl.ds(m, 1)] = main[k, pl.ds(8 * m, 1)]
            rim[k, pl.ds(m + 8, 1)] = main[k, pl.ds(8 * (m + 9) + 7, 1)]


def final_kernel(v0, v1, main, mine, south, north, sums, solution, residual, edge, lay_s, lay_r):
    total = jnp.sum(sums[...], axis=0, keepdims=True)
    lane = lanes(total.shape)
    m = [jnp.sum(jnp.where(lane == k, total, 0.0), axis=1, keepdims=True) for k in range(4)]
    a, c, d = m[1] / m[0], m[2] / m[0], m[3] / m[0]
    step0 = 1.0 / (1.0 + a)
    keep = a * step0
    ratio = (c - a * a) * step0 * step0
    p, s = keep + ratio, -step0
    curvature = p * p + 2.0 * p * s * a + s * s * c + (p * p * a + 2.0 * p * s * c + s * s * d)
    step1 = ratio / curvature
    for_s = (step0 + step1 * p, step1 * s)
    for_r = (keep - step1 * p, s - step1 * (p + s), -(step1 * s))
    depth = solution.shape[0] // (2 * SLAB)
    edge_kernel(mine, south, north, edge)
    for k in range(2 * SLAB + 1):
        for m in range(TILES):
            x0, x1 = v0[k, tile(m)], v1[k, tile(m)]
            x2 = with_rim(main[k, tile(m)], m, edge, k)
            lay_s[pl.ds(m, 8, stride=TILES)] = for_s[0] * x0 + for_s[1] * x1
            lay_r[pl.ds(m, 8, stride=TILES)] = for_r[0] * x0 + for_r[1] * x1 + for_r[2] * x2
        for lay, out in ((lay_s, solution), (lay_r, residual)):
            x = lay[pl.ds(4, BAND)].T
            if k < 2 * SLAB:
                out[pl.ds((k % 2) * depth * SLAB + k // 2, 128, stride=SLAB)] = x
                continue
            for var in (0, 1):
                for l in range(SLAB):
                    row = SHARE * (1 + var) + REST * l
                    out[pl.ds((var * depth + 128) * SLAB + l, REST, stride=SLAB)] = x[row : row + REST]


def shift(x, axis, by):
    n = lax.axis_size(axis)
    return lax.ppermute(x, axis, [(i, (i + by) % n) for i in range(n)])


def far_swap(x):
    n = lax.axis_size("lon")
    return lax.ppermute(x, "lon", [(i, (i + 1 if i % 2 else i - 1) % n) for i in range(n)])


def near_swap(x):
    return lax.ppermute(x, "lon", [(i, i ^ 1) for i in range(lax.axis_size("lon"))])


def body(courant, slot_column_cells, column_counts, innovations, error_weight, weighting):
    depth = courant.shape[2]
    owners = slot_column_cells.shape[2]
    channels = weighting.shape[1]
    slots = owners * SLOTS

    weight = error_weight[:, 0]
    message = jnp.swapaxes(jnp.concatenate([weight * innovations[:, 0], weight], 0), 0, 1)
    sent = lax.all_to_all(
        message.reshape(owners, 2 * NT * SLOTS, channels), ("lon", "lat"), split_axis=0, concat_axis=0, tiled=True
    ).reshape(2 * NT * slots, channels)
    own, own_left, packed, to_near, to_far, edges, table, others = call(
        prepare_kernel,
        [
            (2 * NT * SLAB, ROWS, 128), (2 * NT, ROWS, 128), (2, ROWS, 128), (14, ROWS, 128), (14, ROWS, 128), (26, 8, 128),
            (256, channels), (256, SLAB * channels),
        ],
        [courant.reshape(2 * NT * depth * SLAB, BAND), weighting],
        [pltpu.VMEM((ROWS, 128), F32), pltpu.VMEM((128, 128), F32), pltpu.VMEM((128, 128), F32)],
    )
    c_far, c_near = far_swap(to_far), near_swap(to_near)
    (halo,) = call(halo_kernel, [(26, 8, 128)], [shift(edges, "lat", 1), shift(edges, "lat", -1)])
    index = jnp.swapaxes(slot_column_cells[:, 0], 1, 2)

    parcel = (2 * SLAB + 1, ROWS, 128)
    rim = (2 * SLAB + 1, 16, 128)
    pieces = [(2 * SLAB + 2, ROWS, 128), parcel, parcel]
    steps = [pltpu.VMEM((2 * EXT, ROWS, 128), F32)] * (NT + 1) + [pltpu.VMEM((2, ROWS, 128), F32)] * (NT + 1)

    def gathered(parts, *more):
        mine, to_near, to_far = parts
        return call(gather_kernel, [parcel, rim], [mine, near_swap(to_near), far_swap(to_far), *more])

    def hessian(state, moments, rows):
        main, mine = state
        (edge,) = call(edge_kernel, [rim], [mine, shift(mine, "lat", 1), shift(mine, "lat", -1)])
        return call(
            hessian_kernel,
            [*pieces, parcel, (rows, 128)],
            [
                main, near_swap(main), far_swap(main), edge, near_swap(edge), far_swap(edge),
                weights, table, others, moments, main_c, left_c,
            ],
            [pltpu.VMEM((10 * NT, ROWS, 128), F32), *steps],
        )

    weights, right = call(
        slots_kernel,
        [(NT, SLAB * ROWS, channels), (10 * NT, ROWS, 128)],
        [sent, index, column_counts[:, 0], table, others],
    )
    *parts, main_c, left_c = call(
        right_side_kernel,
        [*pieces, (60, ROWS, 128), (2 * NT, ROWS, 128)],
        [right, own, own_left, packed, c_near, c_far, halo, near_swap(halo), far_swap(halo)],
        [pltpu.VMEM((3, ROWS, 128), F32), *steps],
    )
    *parts, v0, moments = hessian(gathered(parts), jnp.zeros((8, 128), F32), 8)
    *parts, v1, moments = hessian(gathered(parts), moments, owners)
    sums = lax.all_to_all(moments, ("lon", "lat"), split_axis=0, concat_axis=0, tiled=True)
    main, mine = gathered(parts, sums)
    solution, residual = call(
        final_kernel,
        [(2 * depth * SLAB, BAND)] * 2,
        [v0, v1, main, mine, shift(mine, "lat", 1), shift(mine, "lat", -1), sums],
        [pltpu.VMEM(rim, F32), pltpu.VMEM((ROWS, 128), F32), pltpu.VMEM((ROWS, 128), F32)],
    )
    shape = (2, depth, SLAB, BAND)
    return solution.reshape(shape), residual.reshape(shape)


def solution(mesh):
    in_specs = (
        P(None, None, None, "lon", "lat"),
        P(None, ("lon", "lat"), None, None),
        P(None, ("lon", "lat"), None),
        P(None, ("lon", "lat"), None, None, None),
        P(None, ("lon", "lat"), None, None, None),
        P(),
    )
    out_specs = (P(None, None, "lon", "lat"), P(None, None, "lon", "lat"))
    return jax.shard_map(body, mesh=mesh, in_specs=in_specs, out_specs=out_specs, check_vma=False)
```

```python
import functools

import jax
import jax.numpy as jnp
from jax import lax
from jax.experimental import pallas as pl
from jax.experimental.pallas import tpu as pltpu
from jax.sharding import PartitionSpec as P

F32 = jnp.float32
BF16 = jnp.bfloat16
NT = 4
SLAB = 4
BAND = 128
EXT = 3 * SLAB
SLOTS = 4
TILES = 17
ROWS = 8 * TILES
REST = 9
SHARE = SLAB * REST
BASE = (0, 10, 18, 24)
PLANES = {(0, 1): 0, (0, 2): 1, (0, 3): 2, (1, 1): 3, (1, 2): 4, (2, 1): 5}
VMEM = pl.BlockSpec(memory_space=pltpu.VMEM)


def call(kernel, shapes, inputs, scratch=(), flops=0):
    nbytes = sum(x.size * x.dtype.itemsize for x in inputs)
    return pl.pallas_call(
        kernel,
        out_shape=[jax.ShapeDtypeStruct(s, F32) for s in shapes],
        in_specs=[VMEM] * len(inputs),
        out_specs=[VMEM] * len(shapes),
        scratch_shapes=list(scratch),
        compiler_params=pltpu.CompilerParams(vmem_limit_bytes=32 << 20),
        cost_estimate=pl.CostEstimate(flops=flops, bytes_accessed=nbytes, transcendentals=0),
    )(*inputs)


def turn(x, shift):
    shift %= 128
    return pltpu.roll(x, shift, 1) if shift else x


def is_odd():
    return lax.rem(lax.axis_index("lon"), 2) == 1


def has_bands():
    band = lax.axis_index("lat")
    return band > 0, band < lax.axis_size("lat") - 1


def drop(x, by):
    return pltpu.roll(x, by % 8, 0)


def lanes(shape=(8, 128)):
    return lax.broadcasted_iota(jnp.int32, shape, len(shape) - 1)


def depths():
    return lax.broadcasted_iota(jnp.int32, (8, 128), 0)


def tile(m):
    return pl.ds(8 * m, 8)


def parts(u):
    plus = jnp.maximum(u, 0.0)
    return plus, plus - u


def factors(u, v):
    up, um = parts(u)
    vp, vm = parts(v)
    return 1.0 - (up + um) - (vp + vm), up, um, vp, vm


def forward_sweep(main_c, left_c, xs, lefts):
    for t in range(NT):
        src, dst, low, high = xs[t], xs[t + 1], t + 1, 10 - t

        def longitude(e, carry, src=src, dst=dst, first=2 * (1 + BASE[t] - low)):
            k = first + 2 * e
            here = [src[var * EXT + e, tile(0)] for var in (0, 1)]
            start = here
            before = [drop(src[var * EXT + e, tile(TILES - 1)], 1) for var in (0, 1)]
            for m in range(TILES):
                c0, up, um, vp, vm = factors(main_c[k, tile(m)], main_c[k + 1, tile(m)])
                after = [src[var * EXT + e, tile(m + 1)] if m < TILES - 1 else drop(start[var], -1) for var in (0, 1)]
                for var in (0, 1):
                    p = var * EXT + e
                    dst[p, tile(m)] = (
                        c0 * here[var]
                        + (up * src[p - 1, tile(m)] + um * src[p + 1, tile(m)])
                        + (vp * before[var] + vm * after[var])
                    )
                before, here = here, after
            return carry

        lax.fori_loop(low, high + 1, longitude, 0)
        for m in range(TILES):
            c0, up, um, vp, vm = factors(left_c[2 * t, tile(m)], left_c[2 * t + 1, tile(m)])
            for var in (0, 1):
                x = lefts[t][var, tile(m)]
                before = lefts[t][var, tile(m - 1)] if m else drop(lefts[t][var, tile(TILES - 1)], 1)
                after = lefts[t][var, tile(m + 1)] if m < TILES - 1 else drop(lefts[t][var, tile(0)], -1)
                lefts[t + 1][var, tile(m)] = (
                    c0 * x + (up * turn(x, REST) + um * turn(x, -REST)) + (vp * before + vm * after)
                )


def adjoint_lats(terms, write):
    stay0, down0, up0 = terms(0)
    last, up_last, first = None, None, None
    pending, rising = stay0, up0
    for m in range(1, TILES):
        stay, down, up = terms(m)
        done = pending + down
        if m == 1:
            first = done
        else:
            write(m - 1, done)
        pending, rising = stay + rising, up
    write(TILES - 1, pending + drop(down0, -1))
    write(0, first + drop(rising, 1))


def adjoint_sweep(main_c, left_c, grads, ys, lefts):
    for t in reversed(range(NT)):
        src, dst, low, high = ys[t + 1], ys[t], t + 1, 10 - t
        for var in (0, 1):
            for l in range(SLAB):
                g = grads[10 * t + 2 * l + var]
                own = var * EXT + SLAB + l
                src[own] = g if t == NT - 1 else src[own] + g
            g = grads[10 * t + 8 + var]
            lefts[t + 1][var] = g if t == NT - 1 else lefts[t + 1][var] + g
            for e in (low - 1, high + 1):
                src[var * EXT + e] = jnp.zeros((ROWS, 128), F32)

        first_plane = 2 * (1 + BASE[t] - low)

        def longitude(e, carry, src=src, dst=dst, first=first_plane):
            k = first + 2 * e
            both = [{}, {}]

            def shared(m):
                if m not in both[0]:
                    from_east = jnp.maximum(main_c[k + 2, tile(m)], 0.0)
                    from_west = jnp.maximum(-main_c[k - 2, tile(m)], 0.0)
                    both[0][m] = (*factors(main_c[k, tile(m)], main_c[k + 1, tile(m)]), from_east, from_west)
                return both[0][m]

            state = [None, None]
            for m in range(TILES):
                c0, _, _, vp, vm, from_east, from_west = shared(m)
                for var in (0, 1):
                    p = var * EXT + e
                    y = src[p, tile(m)]
                    stay = c0 * y + (from_east * src[p + 1, tile(m)] + from_west * src[p - 1, tile(m)])
                    down, up = vp * y, vm * y
                    if m == 0:
                        state[var] = (down, None, stay, up)
                        continue
                    down0, first, pending, rising = state[var]
                    done = pending + down
                    if m == 1:
                        first = done
                    else:
                        dst[p, tile(m - 1)] = done
                    state[var] = (down0, first, stay + rising, up)
            for var in (0, 1):
                down0, first, pending, rising = state[var]
                dst[var * EXT + e, tile(TILES - 1)] = pending + drop(down0, -1)
                dst[var * EXT + e, tile(0)] = first + drop(rising, 1)
            return carry

        lax.fori_loop(low, high + 1, longitude, 0)
        for m in range(TILES):
            west = jnp.maximum(main_c[first_plane + 2 * low, tile(m)], 0.0)
            east = jnp.maximum(-main_c[first_plane + 2 * high, tile(m)], 0.0)
            for var in (0, 1):
                dst[var * EXT + low - 1, tile(m)] = west * src[var * EXT + low, tile(m)]
                dst[var * EXT + high + 1, tile(m)] = east * src[var * EXT + high, tile(m)]
        for var in (0, 1):

            def terms(m, var=var, t=t):
                c0, up, um, vp, vm = factors(left_c[2 * t, tile(m)], left_c[2 * t + 1, tile(m)])
                y = lefts[t + 1][var, tile(m)]
                return c0 * y + (turn(up * y, -REST) + turn(um * y, REST)), vp * y, vm * y

            def write(m, x, var=var, t=t):
                lefts[t][var, tile(m)] = x

            adjoint_lats(terms, write)


def adjoint_outputs(odd, y, left, out_own, out_near, out_far):
    for var in (0, 1):
        for l in range(SLAB):
            k, p = 2 * l + var, var * EXT + l
            west, east = y[p], y[p + 2 * SLAB]
            out_own[k] = y[p + SLAB]
            out_near[k] = jnp.where(odd, west, east)
            out_far[k] = jnp.where(odd, east, west)
        out_own[2 * SLAB + var] = left[var]
    lane = lanes((ROWS, 128))
    west = jnp.where(lane < SHARE, left[0], turn(left[1], SHARE))
    east = jnp.where(lane < SHARE, turn(left[0], -2 * SHARE), turn(left[1], -SHARE))
    out_near[2 * SLAB] = jnp.where(odd, west, east)
    out_far[2 * SLAB] = jnp.where(odd, east, west)


def with_rim(x, m, rim, plane):
    if m < 8:
        return jnp.where(depths() == 0, rim[plane, pl.ds(m, 1)], x)
    if m > 8:
        return jnp.where(depths() == 7, rim[plane, pl.ds(m - 1, 1)], x)
    return x


def inside(m):
    return depths() != (0 if m < 4 else 7 if m >= TILES - 4 else -1)


def halves(x):
    big = x.astype(BF16)
    return big, (x - big.astype(F32)).astype(BF16)


def dot(a, b, across=False):
    dims = (((1,), (1 if across else 0,)), ((), ()))
    return lax.dot_general(a, b, dims, preferred_element_type=F32)


def split_dot(a, b_big, b_small, across=False):
    a_big, a_small = halves(a)
    return dot(a_big, b_big, across) + (dot(a_small, b_big, across) + dot(a_big, b_small, across))


def spread(values, table, others, grads, t):
    main = split_dot(values, *table, True)
    rest = split_dot(jnp.concatenate([values[l * ROWS : (l + 1) * ROWS] for l in range(SLAB)], 1), *others, True)
    for var in (0, 1):
        for l in range(SLAB):
            grads[10 * t + 2 * l + var] = main[l * ROWS : (l + 1) * ROWS, 128 * var : 128 * (var + 1)]
        grads[10 * t + 8 + var] = rest[:, 128 * var : 128 * (var + 1)]


def observe(x, left, table, others):
    rows = [jnp.concatenate([x[SLAB + l], x[EXT + SLAB + l]], 1) for l in range(SLAB)]
    main = split_dot(jnp.concatenate(rows, 0), *table)
    rest = split_dot(jnp.concatenate([left[0], left[1]], 1), *others)
    return main + jnp.concatenate([rest[:, 128 * l : 128 * (l + 1)] for l in range(SLAB)], 0)


def prepare_kernel(courant, weighting, own, own_left, out_packed, to_near, to_far, edges, table, others, *scratch):
    lay, mine, packed = scratch
    depth = courant.shape[0] // (2 * NT * SLAB)
    main = depth - REST
    odd = is_odd()
    lay[...] = jnp.zeros(lay.shape, F32)
    mine[...] = jnp.zeros(mine.shape, F32)
    packed[...] = jnp.zeros(packed.shape, F32)

    def place(x, target, plane, edge):
        if edge is not None:
            edges[edge, pl.ds(0, 4)] = x[:4]
            edges[edge, pl.ds(4, 4)] = x[BAND - 4 :]
        lay[pl.ds(4, BAND)] = x
        for m in range(TILES):
            target[plane, tile(m)] = lay[pl.ds(m, 8, stride=TILES)]

    for k in (0, 1):
        for t in range(NT):
            for l in range(SLAB):
                start = (2 * t + k) * depth * SLAB + l
                x = courant[pl.ds(start, main, stride=SLAB)]
                place(x.T, own, 8 * t + 4 * k + l, 2 * (4 * t + l) + k if t < NT - 1 else None)
                x = courant[pl.ds(start + main * SLAB, REST, stride=SLAB)]
                mine[pl.ds((SLAB + l) * REST, REST)] = x
                if t < NT - 1:
                    packed[pl.ds(t * SHARE + l * REST, REST)] = x
            place(mine[...].T, own_left, 2 * t + k, None)
            for d in range(1, NT - t):
                west, east = own[8 * t + 4 * k + d - 1], own[8 * t + 4 * k + SLAB - d]
                to_near[2 * PLANES[t, d] + k] = jnp.where(odd, west, east)
                to_far[2 * PLANES[t, d] + k] = jnp.where(odd, east, west)
        place(packed[...].T, out_packed, k, 24 + k)
        to_near[12 + k] = out_packed[k]
        to_far[12 + k] = out_packed[k]
    others[...] = jnp.zeros(others.shape, F32)
    for var in (0, 1):
        table[pl.ds(128 * var, main)] = weighting[pl.ds(depth * var, main)]
        rest = weighting[pl.ds(depth * var + main, REST)]
        for l in range(SLAB):
            others[pl.ds(128 * var + (SLAB + l) * REST, REST), pl.ds(128 * l, 128)] = rest


def halo_kernel(south, north, halo):
    row = depths()
    has_south, has_north = has_bands()
    for k in range(south.shape[0]):
        below = jnp.where(has_south, drop(south[k], 4), 0.0)
        above = jnp.where(has_north, drop(north[k], 4), 0.0)
        halo[k] = jnp.where(row < 4, below, above)


def complete(mine, south, north, k):
    has_south, has_north = has_bands()
    low = jnp.where(has_south, south[k, pl.ds(8, 8)], 0.0) + mine[k, pl.ds(0, 8)]
    high = jnp.where(has_north, north[k, pl.ds(0, 8)], 0.0) + mine[k, pl.ds(8, 8)]
    row = depths()
    return (
        jnp.where(row < 4, jnp.where(has_south, low, 0.0), low),
        jnp.where(row < 4, high, jnp.where(has_north, high, 0.0)),
    )


def edge_kernel(mine, south, north, edge):
    for k in range(edge.shape[0]):
        low, high = complete(mine, south, north, k)
        edge[k, pl.ds(0, 8)] = low
        edge[k, pl.ds(8, 8)] = high


def slots_kernel(sent, index, counts, table, others, weights, grads):
    table, others = halves(table[...]), halves(others[...])
    owners = counts.shape[1]
    shape = (SLAB, TILES, 8, owners)
    l, m, s = (lax.broadcasted_iota(jnp.int32, shape, axis) for axis in range(3))
    latitude = TILES * s + m - 4
    cell = jnp.where((latitude >= 0) & (latitude < BAND), l * BAND + latitude, -2).reshape(SLAB * ROWS, owners)
    for t in range(NT):
        hits, bigs, smalls = [], [], []
        for c in range(SLOTS):
            slot = jnp.where(c < counts[pl.ds(t, 1), :], index[t, pl.ds(c, 1), :], -1)
            hits.append(jnp.where(cell == slot, 1.0, 0.0).astype(BF16))
            both = [sent[pl.ds((i * NT + t) * SLOTS + c, owners, stride=2 * NT * SLOTS)] for i in (0, 1)]
            big, small = halves(jnp.concatenate(both, 1))
            bigs.append(big)
            smalls.append(small)
        hit = jnp.concatenate(hits, 1)
        total = dot(hit, jnp.concatenate(bigs, 0)) + dot(hit, jnp.concatenate(smalls, 0))
        weights[t] = total[:, 128:]
        spread(total[:, :128], table, others, grads, t)


def right_side_kernel(grads, own, own_left, packed, near, far, halo, halo_near, halo_far, *rest):
    out_own, out_near, out_far, main_c, left_c, whole, *scratch = rest
    odd = is_odd()
    lane, row = lanes(), depths()

    def tiles(target, plane, tile_of, halo_of):
        for m in range(TILES):
            x = tile_of(m)
            if halo_of is not None and m < 4:
                x = jnp.where(row == 0, halo_of(m), x)
            if halo_of is not None and m >= TILES - 4:
                x = jnp.where(row == 7, halo_of(m - (TILES - 8)), x)
            target[plane, tile(m)] = x

    for k in (0, 1):
        main_c[k] = jnp.zeros((ROWS, 128), F32)
        main_c[58 + k] = jnp.zeros((ROWS, 128), F32)
        for t in range(NT):
            for e in range(t + 1, 11 - t):
                plane = 2 * (1 + BASE[t] + e - t - 1) + k
                strip = 2 * (4 * t + e % SLAB) + k
                if SLAB <= e < 2 * SLAB:
                    source = 8 * t + 4 * k + e - SLAB
                    tiles(
                        main_c, plane, lambda m, p=source: own[p, tile(m)],
                        (lambda i, p=strip: halo[p, pl.ds(i, 1)]) if t < NT - 1 else None,
                    )
                    continue
                source = 2 * PLANES[t, SLAB - e if e < SLAB else e - 2 * SLAB + 1] + k
                a, b, ha, hb = (near, far, halo_near, halo_far) if e < SLAB else (far, near, halo_far, halo_near)
                tiles(
                    main_c, plane,
                    lambda m, p=source, a=a, b=b: jnp.where(odd, a[p, tile(m)], b[p, tile(m)]),
                    lambda i, p=strip, a=ha, b=hb: jnp.where(odd, a[p, pl.ds(i, 1)], b[p, pl.ds(i, 1)]),
                )
        tiles(whole, 0, lambda m: packed[k, tile(m)], lambda i: halo[24 + k, pl.ds(i, 1)])
        for part, (a, b, ha, hb) in ((1, (near, far, halo_near, halo_far)), (2, (far, near, halo_far, halo_near))):
            tiles(
                whole, part,
                lambda m, a=a, b=b: jnp.where(odd, a[12 + k, tile(m)], b[12 + k, tile(m)]),
                lambda i, a=ha, b=hb: jnp.where(odd, a[24 + k, pl.ds(i, 1)], b[24 + k, pl.ds(i, 1)]),
            )
        for t in range(NT):
            for m in range(TILES):
                if t == NT - 1:
                    left_c[2 * t + k, tile(m)] = own_left[2 * t + k, tile(m)]
                    continue
                mid, west, east = (whole[i, tile(m)] for i in range(3))
                x = jnp.where(lane < SHARE, turn(west, -SHARE * t), turn(mid, SHARE - SHARE * t))
                x = jnp.where(lane < 2 * SHARE, x, turn(east, 2 * SHARE - SHARE * t))
                left_c[2 * t + k, tile(m)] = jnp.where(lane < 3 * SHARE, x, 0.0)
    ys, lefts = scratch[: NT + 1], scratch[NT + 1 :]
    adjoint_sweep(main_c, left_c, grads, ys, lefts)
    adjoint_outputs(odd, ys[0], lefts[0], out_own, out_near, out_far)


def hessian_kernel(own, near, far, e_own, e_near, e_far, weights, table, others, moments, main_c, left_c, *rest):
    out_own, out_near, out_far, out_field, out_moments, grads, *scratch = rest
    xs, lefts = scratch[: NT + 1], scratch[NT + 1 :]
    odd = is_odd()
    lane = lanes()
    square = jnp.zeros((8, 128), F32)
    for m in range(TILES):
        for k in range(2 * SLAB + 1):
            a = with_rim(own[k, tile(m)], m, e_own, k)
            b = with_rim(near[k, tile(m)], m, e_near, k)
            c = with_rim(far[k, tile(m)], m, e_far, k)
            west, east = jnp.where(odd, b, c), jnp.where(odd, c, b)
            out_field[k, tile(m)] = a
            counted = inside(m)
            if k < 2 * SLAB:
                p = (k % 2) * EXT + k // 2
                for i, x in enumerate((west, a, east)):
                    xs[0][p + SLAB * i, tile(m)] = x
            else:
                counted = counted & (lane >= SHARE) & (lane < 3 * SHARE)
                for var in (0, 1):
                    x = jnp.where(lane < SHARE, turn(west, -SHARE * (1 + var)), turn(a, -SHARE * var))
                    x = jnp.where(lane < 2 * SHARE, x, turn(east, SHARE - SHARE * var))
                    lefts[0][var, tile(m)] = jnp.where(lane < 3 * SHARE, x, 0.0)
            square = square + jnp.where(counted, a * a, 0.0)
    forward_sweep(main_c, left_c, xs, lefts)
    table, others = halves(table[...]), halves(others[...])
    product = jnp.zeros((8, 128), F32)
    for t in range(NT):
        seen = observe(xs[t + 1], lefts[t + 1], table, others)
        weighed = weights[t] * seen
        product = product + jnp.sum((weighed * seen).reshape(-1, 8, 128), axis=0)
        spread(weighed, table, others, grads, t)
    lane = lanes(out_moments.shape)
    before = moments[pl.ds(0, 1), :]
    found = jnp.where(lane == 2, jnp.sum(square), jnp.where(lane == 3, jnp.sum(product), 0.0))
    out_moments[...] = jnp.where(lane < 2, turn(jnp.broadcast_to(before, lane.shape), -2), found)
    adjoint_sweep(main_c, left_c, grads, xs, lefts)
    adjoint_outputs(odd, xs[0], lefts[0], out_own, out_near, out_far)


def gather_kernel(own, near, far, *rest):
    main, rim = rest[-2:]
    lane = lanes()
    for k in range(2 * SLAB + 1):
        for m in range(TILES):
            if k < 2 * SLAB:
                x = own[k, tile(m)] + (near[k, tile(m)] + far[k, tile(m)])
            else:
                more = near[k, tile(m)] + far[k, tile(m)]
                first = own[k, tile(m)] + turn(more, SHARE)
                second = own[k + 1, tile(m)] + more
                x = jnp.where(lane < 2 * SHARE, first, turn(second, SHARE))
                x = jnp.where((lane >= SHARE) & (lane < 3 * SHARE), x, 0.0)
            main[k, tile(m)] = x
        for m in range(8):
            rim[k, pl.ds(m, 1)] = main[k, pl.ds(8 * m, 1)]
            rim[k, pl.ds(m + 8, 1)] = main[k, pl.ds(8 * (m + 9) + 7, 1)]


def last_gather_kernel(own, near, far, sums, main, rim, part):
    gather_kernel(own, near, far, main, rim)
    total = jnp.broadcast_to(jnp.sum(sums[...], axis=0, keepdims=True), part.shape)
    part[...] = total
    rim[2 * SLAB + 1] = jnp.broadcast_to(total[:1], rim.shape[1:])


def final_kernel(v0, v1, main, mine, south, north, across, solution, residual, edge, lay_s, lay_r):
    k = 2 * SLAB + 1
    total = (mine[k, pl.ds(0, 1)] + across[pl.ds(0, 1)]) + (south[k, pl.ds(0, 1)] + north[k, pl.ds(0, 1)])
    lane = lanes(total.shape)
    m = [jnp.sum(jnp.where(lane == k, total, 0.0), axis=1, keepdims=True) for k in range(4)]
    a, c, d = m[1] / m[0], m[2] / m[0], m[3] / m[0]
    step0 = 1.0 / (1.0 + a)
    keep = a * step0
    ratio = (c - a * a) * step0 * step0
    p, s = keep + ratio, -step0
    curvature = p * p + 2.0 * p * s * a + s * s * c + (p * p * a + 2.0 * p * s * c + s * s * d)
    step1 = ratio / curvature
    for_s = (step0 + step1 * p, step1 * s)
    for_r = (keep - step1 * p, s - step1 * (p + s), -(step1 * s))
    depth = solution.shape[0] // (2 * SLAB)
    edge_kernel(mine, south, north, edge)
    for k in range(2 * SLAB + 1):
        for m in range(TILES):
            x0, x1 = v0[k, tile(m)], v1[k, tile(m)]
            x2 = with_rim(main[k, tile(m)], m, edge, k)
            lay_s[pl.ds(m, 8, stride=TILES)] = for_s[0] * x0 + for_s[1] * x1
            lay_r[pl.ds(m, 8, stride=TILES)] = for_r[0] * x0 + for_r[1] * x1 + for_r[2] * x2
        for lay, out in ((lay_s, solution), (lay_r, residual)):
            x = lay[pl.ds(4, BAND)].T
            if k < 2 * SLAB:
                out[pl.ds((k % 2) * depth * SLAB + k // 2, 128, stride=SLAB)] = x
                continue
            for var in (0, 1):
                for l in range(SLAB):
                    row = SHARE * (1 + var) + REST * l
                    out[pl.ds((var * depth + 128) * SLAB + l, REST, stride=SLAB)] = x[row : row + REST]


def shift(x, axis, by):
    n = lax.axis_size(axis)
    return lax.ppermute(x, axis, [(i, (i + by) % n) for i in range(n)])


def far_swap(x):
    n = lax.axis_size("lon")
    return lax.ppermute(x, "lon", [(i, (i + 1 if i % 2 else i - 1) % n) for i in range(n)])


def near_swap(x):
    return lax.ppermute(x, "lon", [(i, i ^ 1) for i in range(lax.axis_size("lon"))])


def body(courant, slot_column_cells, column_counts, innovations, error_weight, weighting):
    depth = courant.shape[2]
    owners = slot_column_cells.shape[2]
    channels = weighting.shape[1]
    slots = owners * SLOTS

    weight = error_weight[:, 0]
    message = jnp.swapaxes(jnp.concatenate([weight * innovations[:, 0], weight], 0), 0, 1)
    sent = lax.all_to_all(
        message.reshape(owners, 2 * NT * SLOTS, channels), ("lon", "lat"), split_axis=0, concat_axis=0, tiled=True
    ).reshape(2 * NT * slots, channels)
    own, own_left, packed, to_near, to_far, edges, table, others = call(
        prepare_kernel,
        [
            (2 * NT * SLAB, ROWS, 128), (2 * NT, ROWS, 128), (2, ROWS, 128), (14, ROWS, 128), (14, ROWS, 128), (26, 8, 128),
            (256, channels), (256, SLAB * channels),
        ],
        [courant.reshape(2 * NT * depth * SLAB, BAND), weighting],
        [pltpu.VMEM((ROWS, 128), F32), pltpu.VMEM((128, 128), F32), pltpu.VMEM((128, 128), F32)],
    )
    c_far, c_near = far_swap(to_far), near_swap(to_near)
    (halo,) = call(halo_kernel, [(26, 8, 128)], [shift(edges, "lat", 1), shift(edges, "lat", -1)])
    index = jnp.swapaxes(slot_column_cells[:, 0], 1, 2)

    parcel = (2 * SLAB + 1, ROWS, 128)
    rim = (2 * SLAB + 1, 16, 128)
    pieces = [(2 * SLAB + 2, ROWS, 128), parcel, parcel]
    steps = [pltpu.VMEM((2 * EXT, ROWS, 128), F32)] * (NT + 1) + [pltpu.VMEM((2, ROWS, 128), F32)] * (NT + 1)

    def gathered(parts):
        mine, to_near, to_far = parts
        return call(gather_kernel, [parcel, rim], [mine, near_swap(to_near), far_swap(to_far)])

    def hessian(state, moments, rows):
        main, mine = state
        (edge,) = call(edge_kernel, [rim], [mine, shift(mine, "lat", 1), shift(mine, "lat", -1)])
        return call(
            hessian_kernel,
            [*pieces, parcel, (rows, 128)],
            [
                main, near_swap(main), far_swap(main), edge, near_swap(edge), far_swap(edge),
                weights, table, others, moments, main_c, left_c,
            ],
            [pltpu.VMEM((10 * NT, ROWS, 128), F32), *steps],
        )

    weights, right = call(
        slots_kernel,
        [(NT, SLAB * ROWS, channels), (10 * NT, ROWS, 128)],
        [sent, index, column_counts[:, 0], table, others],
    )
    *parts, main_c, left_c = call(
        right_side_kernel,
        [*pieces, (60, ROWS, 128), (2 * NT, ROWS, 128)],
        [right, own, own_left, packed, c_near, c_far, halo, near_swap(halo), far_swap(halo)],
        [pltpu.VMEM((3, ROWS, 128), F32), *steps],
    )
    *parts, v0, moments = hessian(gathered(parts), jnp.zeros((8, 128), F32), 8)
    *parts, v1, moments = hessian(gathered(parts), moments, lax.axis_size("lon"))
    sums = lax.all_to_all(moments, "lon", split_axis=0, concat_axis=0, tiled=True)
    mine, to_near, to_far = parts
    main, mine, part = call(
        last_gather_kernel,
        [parcel, (2 * SLAB + 2, 16, 128), (8, 128)],
        [mine, near_swap(to_near), far_swap(to_far), sums],
    )
    solution, residual = call(
        final_kernel,
        [(2 * depth * SLAB, BAND)] * 2,
        [v0, v1, main, mine, shift(mine, "lat", 1), shift(mine, "lat", -1), shift(part, "lat", 2)],
        [pltpu.VMEM(rim, F32), pltpu.VMEM((ROWS, 128), F32), pltpu.VMEM((ROWS, 128), F32)],
    )
    shape = (2, depth, SLAB, BAND)
    return solution.reshape(shape), residual.reshape(shape)


def solution(mesh):
    in_specs = (
        P(None, None, None, "lon", "lat"),
        P(None, ("lon", "lat"), None, None),
        P(None, ("lon", "lat"), None),
        P(None, ("lon", "lat"), None, None, None),
        P(None, ("lon", "lat"), None, None, None),
        P(),
    )
    out_specs = (P(None, None, "lon", "lat"), P(None, None, "lon", "lat"))
    return jax.shard_map(body, mesh=mesh, in_specs=in_specs, out_specs=out_specs, check_vma=False)
```
